32 devices in a mesh: seq: 32 (over z, y, x, core), rep: 1.
Axes of the slice: x: 2, y: 2, z: 4, core: 2. Of those that a mesh axis runs over, the one named last changes fastest.
Arguments:
- layer_input: bfloat16 [1, 128, 256, 1024], P('rep', 'seq'), may hold values from -6 to 6
- out_grad: bfloat16 [1, 128, 256, 1024], P('rep', 'seq'), may hold values from -6 to 6
- slot_frame: int32 [1, 128], P('rep'), may hold values from 0 to 127, each once within a row
- ln_gain: float32 [1024], replicated, may hold values from 0.5 to 1.5
- ln_bias: float32 [1024], replicated, may hold values from -3 to 3
- w_qkv: bfloat16 [1024, 3072], replicated, may hold values from -0.1875 to 0.1875
- w_out: bfloat16 [1024, 1024], replicated, may hold values from -0.1875 to 0.1875
- time_bias: float32 [16, 255], replicated, may hold values from -4 to 240
Outputs:
- in_grad: bfloat16 [1, 128, 256, 1024], P('rep', 'seq')
- qkv_grad: float32 [1024, 3072], P(('seq', 'rep'))
- proj_grad: float32 [1024, 1024], P(('seq', 'rep'))
- gain_grad: float32 [1024], P(('seq', 'rep'))
- bias_grad: float32 [1024], P(('seq', 'rep'))
The draws below stay inside these ranges and needn't reach their ends.
Inputs may be any that keep to these rules, and one draw needn't show every extreme that they name: For each video, slot_frame is a permutation of the frames 0 to 127.
All inputs are finite; a program needn't handle non-finite values.
Results may differ from the reference program's by a relative error of at most 0.0094.
Values may be sent and summed in bfloat16 or wider, within the bound.
A program may use at most 192 MiB of HBM per device.

```python
import math
import jax
import jax.numpy as jnp
from jax import lax

D = 1024
HEADS = 16
PATCHES = 256
VIDEOS = 1
FRAMES = 128


def draw_time_bias(key, part):
    key = jax.random.fold_in(key, 11)
    base_bias = jnp.clip(jax.random.normal(key, (HEADS, 2 * FRAMES - 1), jnp.float32), -4.0, 4.0)
    return base_bias


def spiked(drawn, own_key, source, target, parts, factor):
    owner, partner = [(jnp.arange(drawn.shape[dim]) // (drawn.shape[dim] // parts)).reshape([-1 if axis == dim else 1 for axis in range(drawn.ndim)]) for dim in (source, target)]
    chosen = jax.random.permutation(own_key, parts)[partner]
    strong = (owner == chosen) | (owner == (partner + parts // 2) % parts)
    return jnp.where(strong, factor * drawn, drawn)


def levels(own_key, extent, cuts, smallest, high):
    level = 1.0
    for dim, parts in cuts:
        heights = jax.random.uniform(jax.random.fold_in(jax.random.fold_in(own_key, 6), dim), (parts,), jnp.float32, smallest / len(cuts), high / len(cuts))
        level = level * jnp.repeat(jnp.exp(heights), extent[dim] // parts).reshape((-1,) + (1,) * (len(extent) - 1 - dim))
    return level


def gaussian(own_key, dims, width, limit, split=(), held_as=jnp.bfloat16):
    values = jax.random.normal(own_key, dims, jnp.float32) * width
    if len(split) > 0:
        values = levels(own_key, dims, split, -0.22, 0.18) * values
    return jnp.clip(values, min=-limit, max=limit).astype(held_as)


def heavy_noise(stream_key, extent, spread, most, cuts, heavy, kind=jnp.bfloat16):
    entries = spread * jax.random.normal(stream_key, extent, jnp.float32)
    if cuts:
        entries = entries * levels(stream_key, extent, cuts, -0.22, 0.18)
    return jnp.clip(spiked(entries, jax.random.fold_in(stream_key, 3), *heavy), -most, most).astype(kind)


def setup_inputs(seed: int = 0) -> dict:
    key_list = jax.random.split(jax.random.key(seed), 9)
    layer_input = heavy_noise(key_list[0], (VIDEOS, FRAMES, PATCHES, D), 1.0, 6.0, ((1, 32),), (1, 3, 32, 2.75))
    out_grad = heavy_noise(key_list[1], (VIDEOS, FRAMES, PATCHES, D), 1.0, 6.0, ((1, 32),), (1, 3, 32, 2.75))
    slot_frame = jax.vmap(lambda own: jax.random.permutation(own, FRAMES))(jax.random.split(key_list[2], VIDEOS)).reshape((VIDEOS, FRAMES)).astype(jnp.int32)
    ln_gain = jnp.clip(1.0 + 0.1 * jax.random.normal(key_list[3], (D,), jnp.float32), 0.5, 1.5)
    ln_bias = gaussian(key_list[4], (D,), 0.5, 3.0, (), jnp.float32)
    w_qkv = gaussian(key_list[5], (D, 3 * D), D ** -0.5, 0.1875)
    w_out = gaussian(key_list[6], (D, D), D ** -0.5, 0.1875)
    time_bias = draw_time_bias(jax.random.fold_in(key_list[8], 71), 0)
    return {"layer_input": layer_input, "out_grad": out_grad, "slot_frame": slot_frame, "ln_gain": ln_gain, "ln_bias": ln_bias, "w_qkv": w_qkv, "w_out": w_out, "time_bias": time_bias}


def widen(array):
    return array.astype(jnp.float32)

def expand_bias(time_bias, frames):
    offsets = (jnp.arange(frames, dtype=jnp.int32)[None, :] - jnp.arange(frames, dtype=jnp.int32)[:, None] + frames - 1).astype(jnp.int32)
    return jnp.take(time_bias, offsets, axis=1)

def position_backward(rows_in, rows_grad, ln_gain, ln_bias, w_qkv, w_out, bias_table):
    frames, positions, model_width = rows_in.shape
    head_count = bias_table.shape[0]
    head_dim = model_width // head_count
    factor = head_dim ** (-0.5)
    values_in = widen(rows_in)
    row_mean = lax.optimization_barrier(jnp.mean(values_in, axis=-1, keepdims=True))
    centred = values_in - row_mean
    inv_std = lax.rsqrt(lax.optimization_barrier(jnp.mean(centred * centred, axis=-1, keepdims=True)) + 1e-05)
    normed = centred * inv_std
    hidden = (normed * ln_gain + ln_bias).astype(jnp.bfloat16)
    flat_hidden = hidden.reshape(frames * positions, model_width)
    projected = jnp.dot(flat_hidden, w_qkv, preferred_element_type=jnp.float32).astype(jnp.bfloat16)
    projected = projected.reshape(frames, positions, 3, head_count, head_dim)
    queries = projected[:, :, 0]
    key_rows = projected[:, :, 1]
    val_rows = projected[:, :, 2]
    scores = jnp.einsum('tphe,sphe->phts', widen(queries), widen(key_rows)) * factor + bias_table[None]
    weights = jax.nn.softmax(scores, axis=-1)
    short_weights = weights.astype(jnp.bfloat16)
    attended = jnp.einsum('phts,sphe->tphe', widen(short_weights), widen(val_rows)).astype(jnp.bfloat16)
    attended = attended.reshape(frames * positions, model_width)
    flat_grad = rows_grad.reshape(frames * positions, model_width)
    att_grad = jnp.dot(flat_grad, w_out.T, preferred_element_type=jnp.float32).astype(jnp.bfloat16)
    att_grad = att_grad.reshape(frames, positions, head_count, head_dim)
    proj_term = jnp.dot(flat_grad.T, attended, preferred_element_type=jnp.float32)
    weight_grad = jnp.einsum('tphe,sphe->phts', widen(att_grad), widen(val_rows))
    value_grad = jnp.einsum('phts,tphe->sphe', widen(short_weights), widen(att_grad)).astype(jnp.bfloat16)
    score_grad = (weights * (weight_grad - lax.optimization_barrier(jnp.sum(weight_grad * weights, axis=-1, keepdims=True))) * factor).astype(jnp.bfloat16)
    query_grad = jnp.einsum('phts,sphe->tphe', widen(score_grad), widen(key_rows)).astype(jnp.bfloat16)
    key_grad = jnp.einsum('phts,tphe->sphe', widen(score_grad), widen(queries)).astype(jnp.bfloat16)
    packed = jnp.stack([query_grad, key_grad, value_grad], axis=2).reshape(frames * positions, 3 * model_width)
    qkv_term = jnp.dot(flat_hidden.T, packed, preferred_element_type=jnp.float32)
    hidden_grad = jnp.dot(packed, w_qkv.T, preferred_element_type=jnp.float32).reshape(frames, positions, model_width)
    gain_term = lax.optimization_barrier(jnp.sum(hidden_grad * normed, axis=(0, 1)))
    bias_term = lax.optimization_barrier(jnp.sum(hidden_grad, axis=(0, 1)))
    scaled = hidden_grad * ln_gain
    norm_grad = inv_std * (scaled - lax.optimization_barrier(jnp.mean(scaled, axis=-1, keepdims=True)) - normed * lax.optimization_barrier(jnp.mean(scaled * normed, axis=-1, keepdims=True)))
    result = (widen(rows_grad) + norm_grad).astype(jnp.bfloat16)
    return (result, qkv_term, proj_term, gain_term, bias_term)

def reference(layer_input, out_grad, slot_frame, ln_gain, ln_bias, w_qkv, w_out, time_bias):
    videos, frames, patches, model_width = layer_input.shape
    bias_table = expand_bias(time_bias, frames)
    frame_order = jnp.arange(frames, dtype=jnp.int32)

    def invert(slot_row):
        return jnp.zeros((frames,), jnp.int32).at[slot_row.astype(jnp.int32)].set(frame_order)
    inverse = jax.vmap(invert)(slot_frame)
    natural = jnp.take_along_axis(out_grad, inverse[:, :, None, None], axis=1)
    block_size = math.gcd(patches, 8)
    groups = patches // block_size

    def to_blocks(array):
        shaped = array.reshape(videos, frames, groups, block_size, model_width)
        return shaped.transpose(0, 2, 1, 3, 4).reshape(videos * groups, frames, block_size, model_width)
    zero_sums = (jnp.zeros((model_width, 3 * model_width), jnp.float32), jnp.zeros((model_width, model_width), jnp.float32), jnp.zeros((model_width,), jnp.float32), jnp.zeros((model_width,), jnp.float32))

    def advance(running, inputs_pair):
        outcome = position_backward(inputs_pair[0], inputs_pair[1], ln_gain, ln_bias, w_qkv, w_out, bias_table)
        updated = tuple((total + term for total, term in zip(running, outcome[1:])))
        return (updated, outcome[0])
    totals, results = lax.scan(advance, zero_sums, (to_blocks(layer_input), to_blocks(natural)))
    in_grad = results.reshape(videos, groups, frames, block_size, model_width).transpose(0, 2, 1, 3, 4).reshape(videos, frames, patches, model_width)
    factor = (videos * frames * patches) ** (-0.5)
    return (in_grad, totals[0] * factor, totals[1] * factor, totals[2] * factor, totals[3] * factor)
```

```python
import functools

import jax
import jax.numpy as jnp
from jax import lax
from jax.experimental import pallas as pl
from jax.experimental.pallas import tpu as pltpu
from jax.sharding import PartitionSpec as P

MESH = pl.DeviceIdType.MESH
CHUNK = 256
TILE = 256
LANES = 128
F32 = jnp.float32
BF16 = jnp.bfloat16


def dot_nn(a, b):
    return jnp.dot(a, b, preferred_element_type=F32)


def dot_nt(a, b):
    return lax.dot_general(a, b, (((1,), (1,)), ((), ())), preferred_element_type=F32)


def dot_tn(a, b):
    return lax.dot_general(a, b, (((0,), (0,)), ((), ())), preferred_element_type=F32)


def block_place(block, order):
    place = 0
    for bit in order:
        place = place * 2 + ((block >> bit) & 1)
    return place


def part_plan(model_width, blocks):
    tiles = 4 * model_width // TILE
    bits = blocks.bit_length() - 1
    rest = list(range(1, bits))
    first = tiles * 5 // 16
    orders = []
    for start in (0, 1, 2):
        turn = rest[start:] + rest[:start]
        orders.append(([0] if bits else []) + turn)
    return [
        (0, first, orders[0]),
        (first, first, orders[1]),
        (2 * first, tiles - 2 * first, orders[2]),
    ]


def compute_kernel(
    frames, positions, blocks, plan, scale,
    x_ref, g_ref, rows_ref, gain_ref, bias_ref, wqkv_ref, wout_ref, tb_ref,
    out_ref, pa_ref, pb_ref, pc_ref,
    table, xsel, hidden_t, grad_t, z, proj, agrad, hg, normed, res, sums,
):
    tokens, width = x_ref.shape
    per = CHUNK // frames
    heads = tb_ref.shape[0]
    head_dim = width // heads
    factor = head_dim ** (-0.5)
    pairs = heads // 2
    span = 2 * frames

    for h in range(heads):
        row = jnp.broadcast_to(tb_ref[h : h + 1, :], (frames, span))
        rolled = pltpu.roll(row, frames + 1, 1, stride=1, stride_axis=0)
        side = (h % 2) * frames
        table[h // 2, :, side : side + frames] = rolled[:, :frames]
    sums[...] = jnp.zeros_like(sums)
    lane = lax.broadcasted_iota(jnp.int32, (1, LANES), 1)
    left = (lane < head_dim).astype(BF16)
    right = (lane >= head_dim).astype(BF16)
    is_left = lane < head_dim

    def chunk(c, carry):
        base = pl.multiple_of(c * CHUNK, CHUNK)
        here = pl.ds(base, CHUNK)
        want = lax.broadcasted_iota(jnp.int32, (CHUNK, tokens), 0) + base
        pick = jnp.where(rows_ref[0:1, :] == want, 1.0, 0.0).astype(BF16)
        xsel[here, :] = pick
        x = dot_nn(pick, x_ref[...])
        mean = jnp.mean(x, axis=-1, keepdims=True)
        centred = x - mean
        inv = lax.rsqrt(jnp.mean(centred * centred, axis=-1, keepdims=True) + 1e-05)
        norm = centred * inv
        normed[...] = norm
        hidden_f = norm * gain_ref[...] + bias_ref[...]
        hidden = hidden_f.astype(BF16)
        hidden_t[:, here] = jnp.transpose(hidden_f).astype(BF16)

        pick_g = jnp.where(rows_ref[1:2, :] == want, 1.0, 0.0).astype(BF16)
        grad_f = dot_nn(pick_g, g_ref[...])
        grad = grad_f.astype(BF16)
        grad_t[:, here] = jnp.transpose(grad_f).astype(BF16)

        def project(j, carry):
            cols = pl.ds(pl.multiple_of(j * TILE, TILE), TILE)
            proj[:, cols] = dot_nn(hidden, wqkv_ref[:, cols]).astype(BF16)
            return carry

        lax.fori_loop(0, 3 * width // TILE, project, 0)

        def back(j, carry):
            cols = pl.ds(pl.multiple_of(j * TILE, TILE), TILE)
            agrad[:, cols] = dot_nt(grad, wout_ref[cols, :]).astype(BF16)
            return carry

        lax.fori_loop(0, width // TILE, back, 0)

        def attend(j, carry):
            at = pl.multiple_of(j * LANES, LANES)
            for p in range(per):
                rows = slice(p * frames, (p + 1) * frames)
                there = pl.ds(base + p * frames, frames)
                q = proj[rows, pl.ds(at, LANES)]
                k = proj[rows, pl.ds(width + at, LANES)]
                v = proj[rows, pl.ds(2 * width + at, LANES)]
                da = agrad[rows, pl.ds(at, LANES)]
                kk = jnp.concatenate([k * left, k * right], axis=0)
                vv = jnp.concatenate([v * left, v * right], axis=0)
                scores = dot_nt(q, kk) * factor + table[j]
                wgrad = dot_nt(da, vv)
                weights, sgrads = [], []
                for side in range(2):
                    s = scores[:, side * frames : (side + 1) * frames]
                    e = jnp.exp(s - jnp.max(s, axis=-1, keepdims=True))
                    w = e * (1.0 / jnp.sum(e, axis=-1, keepdims=True))
                    d = wgrad[:, side * frames : (side + 1) * frames]
                    inner = jnp.sum(d * w, axis=-1, keepdims=True)
                    weights.append(w.astype(BF16))
                    sgrads.append((w * (d - inner) * factor).astype(BF16))
                w2 = jnp.concatenate(weights, axis=1)
                s2 = jnp.concatenate(sgrads, axis=1)
                z[there, pl.ds(3 * width + at, LANES)] = dot_nn(w2, vv).astype(BF16)
                z[there, pl.ds(at, LANES)] = dot_nn(s2, kk).astype(BF16)
                dk = dot_tn(s2, q)
                dv = dot_tn(w2, da)
                z[there, pl.ds(width + at, LANES)] = jnp.where(
                    is_left, dk[:frames], dk[frames:]
                ).astype(BF16)
                z[there, pl.ds(2 * width + at, LANES)] = jnp.where(
                    is_left, dv[:frames], dv[frames:]
                ).astype(BF16)
            return carry

        lax.fori_loop(0, pairs, attend, 0)

        def widen(j, carry):
            cols = pl.ds(pl.multiple_of(j * TILE, TILE), TILE)
            hg[:, cols] = dot_nt(z[here, : 3 * width], wqkv_ref[cols, :])
            return carry

        lax.fori_loop(0, width // TILE, widen, 0)
        hgrad = hg[...]
        norm = normed[...]
        sums[0:1, :] += jnp.sum(hgrad * norm, axis=0, keepdims=True)
        sums[1:2, :] += jnp.sum(hgrad, axis=0, keepdims=True)
        sc = hgrad * gain_ref[...]
        ngrad = inv * (
            sc
            - jnp.mean(sc, axis=-1, keepdims=True)
            - norm * jnp.mean(sc * norm, axis=-1, keepdims=True)
        )
        res[here, :] = (grad_f + ngrad).astype(BF16)
        return carry

    lax.fori_loop(0, tokens // CHUNK, chunk, 0)

    def give_back(j, carry):
        cols = pl.ds(pl.multiple_of(j * TILE, TILE), TILE)
        out_ref[:, cols] = dot_tn(xsel[...], res[:, cols]).astype(BF16)
        return carry

    lax.fori_loop(0, width // TILE, give_back, 0)

    depth = width // blocks
    parts = (pa_ref, pb_ref, pc_ref)
    hidden_tiles = 3 * width // TILE
    for (first, count, order), ref in zip(plan, parts):
        for lo, hi, lhs in (
            (first, min(first + count, hidden_tiles), hidden_t),
            (max(first, hidden_tiles), first + count, grad_t),
        ):
            if hi <= lo:
                continue

            def term(j, carry, lhs=lhs, ref=ref, order=order, first=first):
                cols = pl.ds(pl.multiple_of(j * TILE, TILE), TILE)
                value = (dot_nn(lhs[...], z[:, cols]) * scale).astype(BF16)
                to = pl.ds(pl.multiple_of((j - first) * TILE, TILE), TILE)
                for b in range(blocks):
                    ref[block_place(b, order), :, to] = value[b * depth : (b + 1) * depth]
                return carry

            lax.fori_loop(lo, hi, term, 0)
    extra = (jnp.transpose(sums[...]) * scale).astype(BF16)
    order, wide = plan[0][2], plan[0][1] * TILE
    for b in range(blocks):
        pa_ref[block_place(b, order), :, wide:] = extra[b * depth : (b + 1) * depth]


def reduce_kernel(rep, orders, *refs):
    count = len(orders)
    ins, outs = refs[:count], refs[count : 2 * count]
    work = refs[2 * count : 3 * count]
    land = refs[3 * count : 4 * count]
    send_sem, recv_sem = refs[4 * count :]
    seq_id, rep_id = lax.axis_index("seq"), lax.axis_index("rep")
    me = seq_id * rep + rep_id
    stages = len(orders[0])

    def partner(bit):
        other = me + (1 - 2 * (lax.div(me, 1 << bit) % 2)) * (1 << bit)
        return (lax.div(other, rep), lax.rem(other, rep))

    barrier = pltpu.get_barrier_semaphore()
    for bit in range(stages):
        pl.semaphore_signal(barrier, inc=1, device_id=partner(bit), device_id_type=MESH)
    pl.semaphore_wait(barrier, stages)

    copies = {}
    base = [0] * count
    keeps = {}

    def start(part, stage):
        bit = orders[part][stage]
        mine = lax.div(me, 1 << bit) % 2
        half = ins[part].shape[0] >> (stage + 1)
        source = ins[part] if stage == 0 else work[part]
        at = half * 2 - half
        keeps[part, stage] = base[part] + mine * half
        away = base[part] + (1 - mine) * half
        copy = pltpu.make_async_remote_copy(
            src_ref=source.at[pl.ds(away, half)],
            dst_ref=land[part].at[pl.ds(at, half)],
            send_sem=send_sem.at[part, stage],
            recv_sem=recv_sem.at[part, stage],
            device_id=partner(bit),
            device_id_type=MESH,
        )
        copy.start()
        copies[part, stage] = copy

    def finish(part, stage):
        half = ins[part].shape[0] >> (stage + 1)
        copies[part, stage].wait_recv()
        keep = keeps[part, stage]
        if half == 1:
            total = work[part][keep].astype(F32) + land[part][half].astype(F32)
            outs[part][...] = total
            return
        source = ins[part] if stage == 0 else work[part]
        to = 0 if stage == 0 else keep

        def add(i, carry):
            total = source[keep + i].astype(F32) + land[part][half + i].astype(F32)
            work[part][to + i] = total.astype(BF16)
            return carry

        lax.fori_loop(0, half, add, 0)
        base[part] = to

    for part in range(count):
        start(part, 0)
    for stage in range(stages):
        for part in range(count):
            finish(part, stage)
            if stage + 1 < stages:
                start(part, stage + 1)
    for copy in copies.values():
        copy.wait_send()


VMEM_SPEC = pl.BlockSpec(memory_space=pltpu.VMEM)


def on_device(layer_input, out_grad, slot_frame, ln_gain, ln_bias, w_qkv, w_out, time_bias):
    seq, rep = lax.axis_size("seq"), lax.axis_size("rep")
    _, local_frames, patches, width = layer_input.shape
    frames, positions = local_frames * seq, patches // seq
    tokens = frames * positions
    heads = time_bias.shape[0]
    devices = seq * rep
    kernel_sum = width // devices >= 16
    blocks = devices if kernel_sum else 1
    plan = part_plan(width, blocks)
    scale = float(tokens * devices) ** (-0.5)
    local_in = lax.all_to_all(layer_input, "seq", split_axis=2, concat_axis=1, tiled=True)
    local_grad = lax.all_to_all(out_grad, "seq", split_axis=2, concat_axis=1, tiled=True)
    slots = jnp.arange(frames, dtype=jnp.int32)
    shift = jnp.arange(positions, dtype=jnp.int32) * frames
    rows = jnp.stack(
        [
            (slots[:, None] + shift[None]).reshape(tokens),
            (slot_frame[0][:, None] + shift[None]).reshape(tokens),
        ]
    )
    tb = jnp.pad(time_bias, ((0, 0), (0, 1)))
    depth = width // blocks
    wides = [count * TILE for _, count, _ in plan]
    wides[0] += LANES
    span = 2 * frames
    result, *terms = pl.pallas_call(
        functools.partial(compute_kernel, frames, positions, blocks, plan, scale),
        out_shape=[jax.ShapeDtypeStruct((tokens, width), BF16)]
        + [jax.ShapeDtypeStruct((blocks, depth, wide), BF16) for wide in wides],
        in_specs=[VMEM_SPEC] * 8,
        out_specs=[VMEM_SPEC] * 4,
        scratch_shapes=[
            pltpu.VMEM((heads // 2, frames, span), F32),
            pltpu.VMEM((tokens, tokens), BF16),
            pltpu.VMEM((width, tokens), BF16),
            pltpu.VMEM((width, tokens), BF16),
            pltpu.VMEM((tokens, 4 * width), BF16),
            pltpu.VMEM((CHUNK, 3 * width), BF16),
            pltpu.VMEM((CHUNK, width), BF16),
            pltpu.VMEM((CHUNK, width), F32),
            pltpu.VMEM((CHUNK, width), F32),
            pltpu.VMEM((tokens, width), BF16),
            pltpu.VMEM((LANES, width), F32),
        ],
        compiler_params=pltpu.CompilerParams(vmem_limit_bytes=60 * 2**20),
    )(
        local_in.reshape(tokens, width),
        local_grad.reshape(tokens, width),
        rows,
        ln_gain.reshape(1, width),
        ln_bias.reshape(1, width),
        w_qkv,
        w_out,
        tb,
    )
    in_grad = lax.all_to_all(
        result.reshape(1, frames, positions, width), "seq", split_axis=1, concat_axis=2, tiled=True
    )
    if kernel_sum:
        orders = [order for _, _, order in plan]
        stages = len(orders[0])
        sums = pl.pallas_call(
            functools.partial(reduce_kernel, rep, orders),
            out_shape=[jax.ShapeDtypeStruct((depth, wide), F32) for wide in wides],
            in_specs=[VMEM_SPEC] * 3,
            out_specs=[VMEM_SPEC] * 3,
            scratch_shapes=[pltpu.VMEM((blocks // 2, depth, wide), BF16) for wide in wides]
            + [pltpu.VMEM((blocks, depth, wide), BF16) for wide in wides]
            + [pltpu.SemaphoreType.DMA((3, stages)), pltpu.SemaphoreType.DMA((3, stages))],
            compiler_params=pltpu.CompilerParams(
                collective_id=0, has_side_effects=True, vmem_limit_bytes=48 * 2**20
            ),
        )(*terms)
    else:
        sums = [
            lax.psum_scatter(
                term.reshape(width, -1).astype(F32), ("seq", "rep"), scatter_dimension=0, tiled=True
            )
            for term in terms
        ]
    first = wides[0] - LANES
    joined = jnp.concatenate([sums[0][:, :first], sums[1], sums[2]], axis=1)
    return (
        in_grad,
        joined[:, : 3 * width],
        joined[:, 3 * width :],
        sums[0][:, first],
        sums[0][:, first + 1],
    )


def solution(mesh):
    return jax.shard_map(
        on_device,
        mesh=mesh,
        in_specs=(
            P("rep", "seq", None, None),
            P("rep", "seq", None, None),
            P("rep", None),
            P(),
            P(),
            P(),
            P(),
            P(),
        ),
        out_specs=(
            P("rep", "seq", None, None),
            P(("seq", "rep"), None),
            P(("seq", "rep"), None),
            P(("seq", "rep")),
            P(("seq", "rep")),
        ),
        check_vma=False,
    )
```

```python
import functools

import jax
import jax.numpy as jnp
from jax import lax
from jax.experimental import pallas as pl
from jax.experimental.pallas import tpu as pltpu
from jax.sharding import PartitionSpec as P

MESH = pl.DeviceIdType.MESH
CHUNK = 512
TILE = 256
LANES = 128
F32 = jnp.float32
BF16 = jnp.bfloat16


def dot_nn(a, b):
    return jnp.dot(a, b, preferred_element_type=F32)


def dot_nt(a, b):
    return lax.dot_general(a, b, (((1,), (1,)), ((), ())), preferred_element_type=F32)


def dot_tn(a, b):
    return lax.dot_general(a, b, (((0,), (0,)), ((), ())), preferred_element_type=F32)


def block_place(block, order):
    place = 0
    for bit in order:
        place = place * 2 + ((block >> bit) & 1)
    return place


def part_plan(model_width, blocks):
    tiles = 4 * model_width // TILE
    bits = blocks.bit_length() - 1
    rest = list(range(1, bits))
    first = tiles * 5 // 16
    orders = []
    for start in (0, 1, 2):
        turn = rest[start:] + rest[:start]
        orders.append(([0] if bits else []) + turn)
    return [
        (0, first, orders[0]),
        (first, first, orders[1]),
        (2 * first, tiles - 2 * first, orders[2]),
    ]


def table_kernel(frames, tb_ref, table):
    heads = tb_ref.shape[0]
    span = 2 * frames
    for h in range(heads):
        row = jnp.broadcast_to(tb_ref[h : h + 1, :], (frames, span))
        rolled = pltpu.roll(row, frames + 1, 1, stride=1, stride_axis=0)
        side = (h % 2) * frames
        table[h // 2, :, side : side + frames] = rolled[:, :frames]


def compute_kernel(
    frames, heads,
    x_ref, rows_ref, back_ref, gain_ref, bias_ref, wqkv_ref, wout_ref, table,
    out_ref, hidden_t, grad_t, z, sums,
    xsel, proj, agrad, hg, normed, res,
):
    arrived, width = x_ref.shape
    tokens = back_ref.shape[1]
    step = min(CHUNK, tokens)
    per = step // frames
    head_dim = width // heads
    factor = head_dim ** (-0.5)
    pairs = heads // 2

    sums[...] = jnp.zeros_like(sums)
    lane = lax.broadcasted_iota(jnp.int32, (1, LANES), 1)
    left = (lane < head_dim).astype(BF16)
    right = (lane >= head_dim).astype(BF16)
    is_left = lane < head_dim

    def chunk(c, carry):
        base = pl.multiple_of(c * step, step)
        here = pl.ds(base, step)
        spot = lax.broadcasted_iota(jnp.int32, (step, tokens), 0) + base
        xsel[here, :] = jnp.where(back_ref[...] == spot, 1.0, 0.0).astype(BF16)
        want = lax.broadcasted_iota(jnp.int32, (step, arrived), 0) + base
        pick = jnp.where(rows_ref[0:1, :] == want, 1.0, 0.0).astype(BF16)
        x = dot_nn(pick, x_ref[...])
        mean = jnp.mean(x, axis=-1, keepdims=True)
        centred = x - mean
        inv = lax.rsqrt(jnp.mean(centred * centred, axis=-1, keepdims=True) + 1e-05)
        norm = centred * inv
        normed[...] = norm
        hidden_f = norm * gain_ref[...] + bias_ref[...]
        hidden = hidden_f.astype(BF16)
        hidden_t[:, here] = jnp.transpose(hidden_f).astype(BF16)

        pick_g = jnp.where(rows_ref[1:2, :] == want, 1.0, 0.0).astype(BF16)
        grad_f = dot_nn(pick_g, x_ref[...])
        grad = grad_f.astype(BF16)
        grad_t[:, here] = jnp.transpose(grad_f).astype(BF16)

        def project(j, carry):
            cols = pl.ds(pl.multiple_of(j * TILE, TILE), TILE)
            proj[:, cols] = dot_nn(hidden, wqkv_ref[:, cols]).astype(BF16)
            return carry

        lax.fori_loop(0, 3 * width // TILE, project, 0)

        def back(j, carry):
            cols = pl.ds(pl.multiple_of(j * TILE, TILE), TILE)
            agrad[:, cols] = dot_nt(grad, wout_ref[cols, :]).astype(BF16)
            return carry

        lax.fori_loop(0, width // TILE, back, 0)

        def attend(j, carry):
            at = pl.multiple_of(j * LANES, LANES)
            for p in range(per):
                rows = slice(p * frames, (p + 1) * frames)
                there = pl.ds(base + p * frames, frames)
                q = proj[rows, pl.ds(at, LANES)]
                k = proj[rows, pl.ds(width + at, LANES)]
                v = proj[rows, pl.ds(2 * width + at, LANES)]
                da = agrad[rows, pl.ds(at, LANES)]
                kk = jnp.concatenate([k * left, k * right], axis=0)
                vv = jnp.concatenate([v * left, v * right], axis=0)
                scores = dot_nt(q, kk) * factor + table[j]
                wgrad = dot_nt(da, vv)
                weights, sgrads = [], []
                for side in range(2):
                    s = scores[:, side * frames : (side + 1) * frames]
                    e = jnp.exp(s - jnp.max(s, axis=-1, keepdims=True))
                    w = e * (1.0 / jnp.sum(e, axis=-1, keepdims=True))
                    d = wgrad[:, side * frames : (side + 1) * frames]
                    inner = jnp.sum(d * w, axis=-1, keepdims=True)
                    weights.append(w.astype(BF16))
                    sgrads.append((w * (d - inner) * factor).astype(BF16))
                w2 = jnp.concatenate(weights, axis=1)
                s2 = jnp.concatenate(sgrads, axis=1)
                z[there, pl.ds(3 * width + at, LANES)] = dot_nn(w2, vv).astype(BF16)
                z[there, pl.ds(at, LANES)] = dot_nn(s2, kk).astype(BF16)
                dk = dot_tn(s2, q)
                dv = dot_tn(w2, da)
                z[there, pl.ds(width + at, LANES)] = jnp.where(
                    is_left, dk[:frames], dk[frames:]
                ).astype(BF16)
                z[there, pl.ds(2 * width + at, LANES)] = jnp.where(
                    is_left, dv[:frames], dv[frames:]
                ).astype(BF16)
            return carry

        lax.fori_loop(0, pairs, attend, 0)

        def widen(j, carry):
            cols = pl.ds(pl.multiple_of(j * TILE, TILE), TILE)
            hg[:, cols] = dot_nt(z[here, : 3 * width], wqkv_ref[cols, :])
            return carry

        lax.fori_loop(0, width // TILE, widen, 0)
        hgrad = hg[...]
        norm = normed[...]
        sums[0:1, :] += jnp.sum(hgrad * norm, axis=0, keepdims=True)
        sums[1:2, :] += jnp.sum(hgrad, axis=0, keepdims=True)
        sc = hgrad * gain_ref[...]
        ngrad = inv * (
            sc
            - jnp.mean(sc, axis=-1, keepdims=True)
            - norm * jnp.mean(sc * norm, axis=-1, keepdims=True)
        )
        res[here, :] = (grad_f + ngrad).astype(BF16)
        return carry

    lax.fori_loop(0, tokens // step, chunk, 0)

    def give_back(j, carry):
        cols = pl.ds(pl.multiple_of(j * TILE, TILE), TILE)
        out_ref[:, cols] = dot_tn(xsel[...], res[:, cols]).astype(BF16)
        return carry

    lax.fori_loop(0, width // TILE, give_back, 0)


def weight_kernel(blocks, plan, scale, *refs):
    hidden, grads, zs, sums = refs[0:2], refs[2:4], refs[4:6], refs[6:8]
    pa_ref, pb_ref, pc_ref = refs[8:]
    width = hidden[0].shape[0]
    depth = width // blocks
    parts = (pa_ref, pb_ref, pc_ref)
    hidden_tiles = 3 * width // TILE
    for (first, count, order), ref in zip(plan, parts):
        for lo, hi, lhs in (
            (first, min(first + count, hidden_tiles), hidden),
            (max(first, hidden_tiles), first + count, grads),
        ):
            if hi <= lo:
                continue

            def term(j, carry, lhs=lhs, ref=ref, order=order, first=first):
                cols = pl.ds(pl.multiple_of(j * TILE, TILE), TILE)
                both = [dot_nn(rows[...], z[:, cols]) for rows, z in zip(lhs, zs)]
                value = ((both[0] + both[1]) * scale).astype(BF16)
                to = pl.ds(pl.multiple_of((j - first) * TILE, TILE), TILE)
                for b in range(blocks):
                    ref[block_place(b, order), :, to] = value[b * depth : (b + 1) * depth]
                return carry

            lax.fori_loop(lo, hi, term, 0)
    extra = (jnp.transpose(sums[0][...] + sums[1][...]) * scale).astype(BF16)
    order, wide = plan[0][2], plan[0][1] * TILE
    for b in range(blocks):
        pa_ref[block_place(b, order), :, wide:] = extra[b * depth : (b + 1) * depth]


def reduce_kernel(rep, orders, *refs):
    count = len(orders)
    ins, outs = refs[:count], refs[count : 2 * count]
    work = refs[2 * count : 3 * count]
    land = refs[3 * count : 4 * count]
    send_sem, recv_sem = refs[4 * count :]
    seq_id, rep_id = lax.axis_index("seq"), lax.axis_index("rep")
    me = seq_id * rep + rep_id
    stages = len(orders[0])

    def partner(bit):
        other = me + (1 - 2 * (lax.div(me, 1 << bit) % 2)) * (1 << bit)
        return (lax.div(other, rep), lax.rem(other, rep))

    barrier = pltpu.get_barrier_semaphore()
    for bit in range(stages):
        pl.semaphore_signal(barrier, inc=1, device_id=partner(bit), device_id_type=MESH)
    pl.semaphore_wait(barrier, stages)

    copies = {}
    base = [0] * count
    keeps = {}

    def start(part, stage):
        bit = orders[part][stage]
        mine = lax.div(me, 1 << bit) % 2
        half = ins[part].shape[0] >> (stage + 1)
        source = ins[part] if stage == 0 else work[part]
        at = half * 2 - half
        keeps[part, stage] = base[part] + mine * half
        away = base[part] + (1 - mine) * half
        copy = pltpu.make_async_remote_copy(
            src_ref=source.at[pl.ds(away, half)],
            dst_ref=land[part].at[pl.ds(at, half)],
            send_sem=send_sem.at[part, stage],
            recv_sem=recv_sem.at[part, stage],
            device_id=partner(bit),
            device_id_type=MESH,
        )
        copy.start()
        copies[part, stage] = copy

    def finish(part, stage):
        half = ins[part].shape[0] >> (stage + 1)
        copies[part, stage].wait_recv()
        keep = keeps[part, stage]
        if half == 1:
            total = work[part][keep].astype(F32) + land[part][half].astype(F32)
            outs[part][...] = total
            return
        source = ins[part] if stage == 0 else work[part]
        to = 0 if stage == 0 else keep

        def add(i, carry):
            total = source[keep + i].astype(F32) + land[part][half + i].astype(F32)
            work[part][to + i] = total.astype(BF16)
            return carry

        lax.fori_loop(0, half, add, 0)
        base[part] = to

    for part in range(count):
        start(part, 0)
    for stage in range(stages):
        for part in range(count):
            finish(part, stage)
            if stage + 1 < stages:
                start(part, stage + 1)
    for copy in copies.values():
        copy.wait_send()


VMEM_SPEC = pl.BlockSpec(memory_space=pltpu.VMEM)


def on_device(layer_input, out_grad, slot_frame, ln_gain, ln_bias, w_qkv, w_out, time_bias):
    seq, rep = lax.axis_size("seq"), lax.axis_size("rep")
    _, local_frames, patches, width = layer_input.shape
    frames, positions = local_frames * seq, patches // seq
    tokens = frames * positions
    heads = time_bias.shape[0]
    devices = seq * rep
    kernel_sum = width // devices >= 16
    blocks = devices if kernel_sum else 1
    plan = part_plan(width, blocks)
    scale = float(tokens * devices) ** (-0.5)
    part = positions // 2
    held = tokens // 2
    span = 2 * frames

    def arrange(array):
        shaped = array.reshape(local_frames, seq, 2, part, width).transpose(2, 1, 0, 3, 4)
        return shaped.reshape(2, seq, local_frames * part, width)

    joint = jnp.concatenate([arrange(layer_input), arrange(out_grad)], axis=2)
    slots = jnp.arange(frames, dtype=jnp.int32)
    shift = jnp.arange(part, dtype=jnp.int32) * frames

    def places(at):
        return (at[:, None] + shift[None]).reshape(seq, local_frames * part)

    here = places(slots)
    none = jnp.full_like(here, -1)
    rows = jnp.stack(
        [
            jnp.concatenate([here, none], axis=1).reshape(2 * held),
            jnp.concatenate([none, places(slot_frame[0])], axis=1).reshape(2 * held),
        ]
    )
    table = pl.pallas_call(
        functools.partial(table_kernel, frames),
        out_shape=jax.ShapeDtypeStruct((heads // 2, frames, span), F32),
        in_specs=[VMEM_SPEC],
        out_specs=VMEM_SPEC,
    )(jnp.pad(time_bias, ((0, 0), (0, 1))))
    depth = width // blocks
    wides = [count * TILE for _, count, _ in plan]
    wides[0] += LANES
    step = min(CHUNK, held)
    compute = pl.pallas_call(
        functools.partial(compute_kernel, frames, heads),
        out_shape=[
            jax.ShapeDtypeStruct((held, width), BF16),
            jax.ShapeDtypeStruct((width, held), BF16),
            jax.ShapeDtypeStruct((width, held), BF16),
            jax.ShapeDtypeStruct((held, 4 * width), BF16),
            jax.ShapeDtypeStruct((LANES, width), F32),
        ],
        in_specs=[VMEM_SPEC] * 8,
        out_specs=[VMEM_SPEC] * 5,
        scratch_shapes=[
            pltpu.VMEM((held, held), BF16),
            pltpu.VMEM((step, 3 * width), BF16),
            pltpu.VMEM((step, width), BF16),
            pltpu.VMEM((step, width), F32),
            pltpu.VMEM((step, width), F32),
            pltpu.VMEM((held, width), BF16),
        ],
        compiler_params=pltpu.CompilerParams(vmem_limit_bytes=52 * 2**20),
        cost_estimate=pl.CostEstimate(
            flops=30 * held * width * width, bytes_accessed=24 * 2**20, transcendentals=0
        ),
    )
    results, saved = [], []
    for half in range(2):
        got = lax.all_to_all(joint[half], "seq", split_axis=0, concat_axis=0, tiled=True)
        result, *kept = compute(
            got.reshape(2 * held, width),
            rows,
            here.reshape(1, held),
            ln_gain.reshape(1, width),
            ln_bias.reshape(1, width),
            w_qkv,
            w_out,
            table,
        )
        saved.append(kept)
        results.append(
            lax.all_to_all(
                result.reshape(seq, local_frames * part, width),
                "seq", split_axis=0, concat_axis=0, tiled=True,
            )
        )
    in_grad = (
        jnp.stack(results)
        .reshape(2, seq, local_frames, part, width)
        .transpose(2, 1, 0, 3, 4)
        .reshape(1, local_frames, patches, width)
    )
    terms = pl.pallas_call(
        functools.partial(weight_kernel, blocks, plan, scale),
        out_shape=[jax.ShapeDtypeStruct((blocks, depth, wide), BF16) for wide in wides],
        in_specs=[VMEM_SPEC] * 8,
        out_specs=[VMEM_SPEC] * 3,
        compiler_params=pltpu.CompilerParams(vmem_limit_bytes=40 * 2**20),
    )(*[saved[half][i] for i in range(4) for half in range(2)])
    if kernel_sum:
        orders = [order for _, _, order in plan]
        stages = len(orders[0])
        sums = pl.pallas_call(
            functools.partial(reduce_kernel, rep, orders),
            out_shape=[jax.ShapeDtypeStruct((depth, wide), F32) for wide in wides],
            in_specs=[VMEM_SPEC] * 3,
            out_specs=[VMEM_SPEC] * 3,
            scratch_shapes=[pltpu.VMEM((blocks // 2, depth, wide), BF16) for wide in wides]
            + [pltpu.VMEM((blocks, depth, wide), BF16) for wide in wides]
            + [pltpu.SemaphoreType.DMA((3, stages)), pltpu.SemaphoreType.DMA((3, stages))],
            compiler_params=pltpu.CompilerParams(
                collective_id=0, has_side_effects=True, vmem_limit_bytes=48 * 2**20
            ),
        )(*terms)
    else:
        sums = [
            lax.psum_scatter(
                term.reshape(width, -1).astype(F32), ("seq", "rep"), scatter_dimension=0, tiled=True
            )
            for term in terms
        ]
    first = wides[0] - LANES
    joined = jnp.concatenate([sums[0][:, :first], sums[1], sums[2]], axis=1)
    return (
        in_grad,
        joined[:, : 3 * width],
        joined[:, 3 * width :],
        sums[0][:, first],
        sums[0][:, first + 1],
    )


def solution(mesh):
    return jax.shard_map(
        on_device,
        mesh=mesh,
        in_specs=(
            P("rep", "seq", None, None),
            P("rep", "seq", None, None),
            P("rep", None),
            P(),
            P(),
            P(),
            P(),
            P(),
        ),
        out_specs=(
            P("rep", "seq", None, None),
            P(("seq", "rep"), None),
            P(("seq", "rep"), None),
            P(("seq", "rep")),
            P(("seq", "rep")),
        ),
        check_vma=False,
    )
```

```python
import functools

import jax
import jax.numpy as jnp
import numpy as np
from jax import lax
from jax.experimental import pallas as pl
from jax.experimental.pallas import tpu as pltpu
from jax.sharding import PartitionSpec as P

MESH = pl.DeviceIdType.MESH
CHUNK = 512
TILE = 256
LANES = 128
F32 = jnp.float32
BF16 = jnp.bfloat16


def dot_nn(a, b):
    return jnp.dot(a, b, preferred_element_type=F32)


def dot_nt(a, b):
    return lax.dot_general(a, b, (((1,), (1,)), ((), ())), preferred_element_type=F32)


def dot_tn(a, b):
    return lax.dot_general(a, b, (((0,), (0,)), ((), ())), preferred_element_type=F32)


def block_place(block, order):
    place = 0
    for bit in order:
        place = place * 2 + ((block >> bit) & 1)
    return place


def part_plan(model_width, blocks):
    tiles = 4 * model_width // TILE
    bits = blocks.bit_length() - 1
    rest = list(range(1, bits))
    first = tiles * 5 // 16
    orders = []
    for start in (0, 1, 2):
        turn = rest[start:] + rest[:start]
        orders.append(([0] if bits else []) + turn)
    return [
        (0, first, orders[0]),
        (first, first, orders[1]),
        (2 * first, tiles - 2 * first, orders[2]),
    ]


def arrange_kernel(local_frames, x_ref, g_ref, place_ref, first_ref, second_ref):
    group = place_ref.shape[1] // (2 * local_frames)
    count = place_ref.shape[1]
    spot = lax.broadcasted_iota(jnp.int32, (count, count), 0)
    pick = jnp.where(place_ref[...] == spot, 1.0, 0.0).astype(BF16)
    for g in range(x_ref.shape[1] // group):
        rows = [ref[f, g * group : (g + 1) * group, :] for ref in (x_ref, g_ref) for f in range(local_frames)]
        value = dot_nn(pick, jnp.concatenate(rows, axis=0)).astype(BF16)
        half = count // 2
        first_ref[g * half : (g + 1) * half, :] = value[:half]
        second_ref[g * half : (g + 1) * half, :] = value[half:]


def restore_kernel(local_frames, first_ref, second_ref, place_ref, out_ref):
    count = place_ref.shape[1]
    group, half = count // local_frames, count // 2
    spot = lax.broadcasted_iota(jnp.int32, (count, count), 0)
    pick = jnp.where(place_ref[...] == spot, 1.0, 0.0).astype(BF16)
    for g in range(out_ref.shape[1] // group):
        rows = [ref[g * half : (g + 1) * half, :] for ref in (first_ref, second_ref)]
        value = dot_tn(pick, jnp.concatenate(rows, axis=0)).astype(BF16)
        for f in range(local_frames):
            out_ref[f, g * group : (g + 1) * group, :] = value[f * group : (f + 1) * group]


def row_places(sources, local_frames, group, positions):
    part = positions // 2
    owners = group // positions
    s, f, at = np.meshgrid(np.arange(sources), np.arange(local_frames), np.arange(group), indexing="ij")
    owner, half, p = at // positions, at % positions // part, at % part
    place = (((half * owners + owner) * sources + s) * local_frames + f) * part + p
    return place.reshape(1, -1).astype(np.int32)


def table_kernel(frames, tb_ref, table):
    heads = tb_ref.shape[0]
    span = 2 * frames
    for h in range(heads):
        row = jnp.broadcast_to(tb_ref[h : h + 1, :], (frames, span))
        rolled = pltpu.roll(row, frames + 1, 1, stride=1, stride_axis=0)
        side = (h % 2) * frames
        table[h // 2, :, side : side + frames] = rolled[:, :frames]


def compute_kernel(
    frames, heads,
    x_ref, rows_ref, back_ref, gain_ref, bias_ref, wqkv_ref, wout_ref, table,
    out_ref, hidden_t, grad_t, z, sums,
    xsel, proj, agrad, hg, normed, res,
):
    arrived, width = x_ref.shape
    tokens = back_ref.shape[1]
    step = min(CHUNK, tokens)
    per = step // frames
    head_dim = width // heads
    factor = head_dim ** (-0.5)
    pairs = heads // 2

    sums[...] = jnp.zeros_like(sums)
    lane = lax.broadcasted_iota(jnp.int32, (1, LANES), 1)
    left = (lane < head_dim).astype(BF16)
    right = (lane >= head_dim).astype(BF16)
    is_left = lane < head_dim

    def chunk(c, carry):
        base = pl.multiple_of(c * step, step)
        here = pl.ds(base, step)
        spot = lax.broadcasted_iota(jnp.int32, (step, tokens), 0) + base
        xsel[here, :] = jnp.where(back_ref[...] == spot, 1.0, 0.0).astype(BF16)
        want = lax.broadcasted_iota(jnp.int32, (step, arrived), 0) + base
        pick = jnp.where(rows_ref[0:1, :] == want, 1.0, 0.0).astype(BF16)
        x = dot_nn(pick, x_ref[...])
        mean = jnp.mean(x, axis=-1, keepdims=True)
        centred = x - mean
        inv = lax.rsqrt(jnp.mean(centred * centred, axis=-1, keepdims=True) + 1e-05)
        norm = centred * inv
        normed[...] = norm
        hidden_f = norm * gain_ref[...] + bias_ref[...]
        hidden = hidden_f.astype(BF16)
        hidden_t[:, here] = jnp.transpose(hidden_f).astype(BF16)

        pick_g = jnp.where(rows_ref[1:2, :] == want, 1.0, 0.0).astype(BF16)
        grad_f = dot_nn(pick_g, x_ref[...])
        grad = grad_f.astype(BF16)
        grad_t[:, here] = jnp.transpose(grad_f).astype(BF16)

        def project(j, carry):
            cols = pl.ds(pl.multiple_of(j * TILE, TILE), TILE)
            proj[:, cols] = dot_nn(hidden, wqkv_ref[:, cols]).astype(BF16)
            return carry

        lax.fori_loop(0, 3 * width // TILE, project, 0)

        def back(j, carry):
            cols = pl.ds(pl.multiple_of(j * TILE, TILE), TILE)
            agrad[:, cols] = dot_nt(grad, wout_ref[cols, :]).astype(BF16)
            return carry

        lax.fori_loop(0, width // TILE, back, 0)

        def attend(j, carry):
            at = pl.multiple_of(j * LANES, LANES)
            loaded, scored, soft = [], [], []
            for p in range(per):
                rows = slice(p * frames, (p + 1) * frames)
                q = proj[rows, pl.ds(at, LANES)]
                k = proj[rows, pl.ds(width + at, LANES)]
                v = proj[rows, pl.ds(2 * width + at, LANES)]
                da = agrad[rows, pl.ds(at, LANES)]
                kk = jnp.concatenate([k * left, k * right], axis=0)
                vv = jnp.concatenate([v * left, v * right], axis=0)
                loaded.append((q, da, kk, vv))
                scored.append((dot_nt(q, kk), dot_nt(da, vv)))
            for scores, wgrad in scored:
                scores = scores * factor + table[j]
                weights, sgrads = [], []
                for side in range(2):
                    s = scores[:, side * frames : (side + 1) * frames]
                    e = jnp.exp(s - jnp.max(s, axis=-1, keepdims=True))
                    w = e * (1.0 / jnp.sum(e, axis=-1, keepdims=True))
                    d = wgrad[:, side * frames : (side + 1) * frames]
                    inner = jnp.sum(d * w, axis=-1, keepdims=True)
                    weights.append(w.astype(BF16))
                    sgrads.append((w * (d - inner) * factor).astype(BF16))
                soft.append((jnp.concatenate(weights, axis=1), jnp.concatenate(sgrads, axis=1)))
            for p in range(per):
                (q, da, kk, vv), (w2, s2) = loaded[p], soft[p]
                there = pl.ds(base + p * frames, frames)
                z[there, pl.ds(3 * width + at, LANES)] = dot_nn(w2, vv).astype(BF16)
                z[there, pl.ds(at, LANES)] = dot_nn(s2, kk).astype(BF16)
                dk = dot_tn(s2, q)
                dv = dot_tn(w2, da)
                z[there, pl.ds(width + at, LANES)] = jnp.where(
                    is_left, dk[:frames], dk[frames:]
                ).astype(BF16)
                z[there, pl.ds(2 * width + at, LANES)] = jnp.where(
                    is_left, dv[:frames], dv[frames:]
                ).astype(BF16)
            return carry

        lax.fori_loop(0, pairs, attend, 0)

        def widen(j, carry):
            cols = pl.ds(pl.multiple_of(j * TILE, TILE), TILE)
            hg[:, cols] = dot_nt(z[here, : 3 * width], wqkv_ref[cols, :])
            return carry

        lax.fori_loop(0, width // TILE, widen, 0)
        hgrad = hg[...]
        norm = normed[...]
        sums[0:1, :] += jnp.sum(hgrad * norm, axis=0, keepdims=True)
        sums[1:2, :] += jnp.sum(hgrad, axis=0, keepdims=True)
        sc = hgrad * gain_ref[...]
        ngrad = inv * (
            sc
            - jnp.mean(sc, axis=-1, keepdims=True)
            - norm * jnp.mean(sc * norm, axis=-1, keepdims=True)
        )
        res[here, :] = (grad_f + ngrad).astype(BF16)
        return carry

    lax.fori_loop(0, tokens // step, chunk, 0)

    def give_back(j, carry):
        cols = pl.ds(pl.multiple_of(j * TILE, TILE), TILE)
        out_ref[:, cols] = dot_tn(xsel[...], res[:, cols]).astype(BF16)
        return carry

    lax.fori_loop(0, width // TILE, give_back, 0)


def weight_kernel(blocks, plan, scale, *refs):
    hidden, grads, zs, sums = refs[0:2], refs[2:4], refs[4:6], refs[6:8]
    pa_ref, pb_ref, pc_ref = refs[8:]
    width = hidden[0].shape[0]
    depth = width // blocks
    parts = (pa_ref, pb_ref, pc_ref)
    hidden_tiles = 3 * width // TILE
    for (first, count, order), ref in zip(plan, parts):
        for lo, hi, lhs in (
            (first, min(first + count, hidden_tiles), hidden),
            (max(first, hidden_tiles), first + count, grads),
        ):
            if hi <= lo:
                continue

            def term(j, carry, lhs=lhs, ref=ref, order=order, first=first):
                cols = pl.ds(pl.multiple_of(j * TILE, TILE), TILE)
                both = [dot_nn(rows[...], z[:, cols]) for rows, z in zip(lhs, zs)]
                value = ((both[0] + both[1]) * scale).astype(BF16)
                to = pl.ds(pl.multiple_of((j - first) * TILE, TILE), TILE)
                for b in range(blocks):
                    ref[block_place(b, order), :, to] = value[b * depth : (b + 1) * depth]
                return carry

            lax.fori_loop(lo, hi, term, 0)
    extra = (jnp.transpose(sums[0][...] + sums[1][...]) * scale).astype(BF16)
    order, wide = plan[0][2], plan[0][1] * TILE
    for b in range(blocks):
        pa_ref[block_place(b, order), :, wide:] = extra[b * depth : (b + 1) * depth]


def reduce_kernel(rep, orders, *refs):
    count = len(orders)
    ins, outs = refs[:count], refs[count : 2 * count]
    work = refs[2 * count : 3 * count]
    land = refs[3 * count : 4 * count]
    send_sem, recv_sem = refs[4 * count :]
    seq_id, rep_id = lax.axis_index("seq"), lax.axis_index("rep")
    me = seq_id * rep + rep_id
    stages = len(orders[0])

    def partner(bit):
        other = me + (1 - 2 * (lax.div(me, 1 << bit) % 2)) * (1 << bit)
        return (lax.div(other, rep), lax.rem(other, rep))

    barrier = pltpu.get_barrier_semaphore()
    for bit in range(stages):
        pl.semaphore_signal(barrier, inc=1, device_id=partner(bit), device_id_type=MESH)
    pl.semaphore_wait(barrier, stages)

    copies = {}
    base = [0] * count
    keeps = {}

    def start(part, stage):
        bit = orders[part][stage]
        mine = lax.div(me, 1 << bit) % 2
        half = ins[part].shape[0] >> (stage + 1)
        source = ins[part] if stage == 0 else work[part]
        at = half * 2 - half
        keeps[part, stage] = base[part] + mine * half
        away = base[part] + (1 - mine) * half
        copy = pltpu.make_async_remote_copy(
            src_ref=source.at[pl.ds(away, half)],
            dst_ref=land[part].at[pl.ds(at, half)],
            send_sem=send_sem.at[part, stage],
            recv_sem=recv_sem.at[part, stage],
            device_id=partner(bit),
            device_id_type=MESH,
        )
        copy.start()
        copies[part, stage] = copy

    def finish(part, stage):
        half = ins[part].shape[0] >> (stage + 1)
        copies[part, stage].wait_recv()
        keep = keeps[part, stage]
        if half == 1:
            total = work[part][keep].astype(F32) + land[part][half].astype(F32)
            outs[part][...] = total
            return
        source = ins[part] if stage == 0 else work[part]
        to = 0 if stage == 0 else keep

        def add(i, carry):
            total = source[keep + i].astype(F32) + land[part][half + i].astype(F32)
            work[part][to + i] = total.astype(BF16)
            return carry

        lax.fori_loop(0, half, add, 0)
        base[part] = to

    for part in range(count):
        start(part, 0)
    for stage in range(stages):
        for part in range(count):
            finish(part, stage)
            if stage + 1 < stages:
                start(part, stage + 1)
    for copy in copies.values():
        copy.wait_send()


VMEM_SPEC = pl.BlockSpec(memory_space=pltpu.VMEM)


def on_device(layer_input, out_grad, slot_frame, ln_gain, ln_bias, w_qkv, w_out, time_bias):
    seq, rep = lax.axis_size("seq"), lax.axis_size("rep")
    _, local_frames, patches, width = layer_input.shape
    frames, positions = local_frames * seq, patches // seq
    tokens = frames * positions
    heads = time_bias.shape[0]
    devices = seq * rep
    kernel_sum = width // devices >= 16
    blocks = devices if kernel_sum else 1
    plan = part_plan(width, blocks)
    scale = float(tokens * devices) ** (-0.5)
    part = positions // 2
    held = tokens // 2
    span = 2 * frames

    group = min(patches, 256 // local_frames)
    joint = pl.pallas_call(
        functools.partial(arrange_kernel, local_frames),
        out_shape=[jax.ShapeDtypeStruct((2 * held, width), BF16)] * 2,
        in_specs=[VMEM_SPEC] * 3,
        out_specs=[VMEM_SPEC] * 2,
        compiler_params=pltpu.CompilerParams(vmem_limit_bytes=32 * 2**20),
    )(
        layer_input[0],
        out_grad[0],
        jnp.asarray(row_places(2, local_frames, group, positions)),
    )
    slots = jnp.arange(frames, dtype=jnp.int32)
    shift = jnp.arange(part, dtype=jnp.int32) * frames

    def places(at):
        return (at[:, None] + shift[None]).reshape(seq, local_frames * part)

    here = places(slots)
    none = jnp.full_like(here, -1)
    rows = jnp.stack(
        [
            jnp.concatenate([here, none], axis=1).reshape(2 * held),
            jnp.concatenate([none, places(slot_frame[0])], axis=1).reshape(2 * held),
        ]
    )
    table = pl.pallas_call(
        functools.partial(table_kernel, frames),
        out_shape=jax.ShapeDtypeStruct((heads // 2, frames, span), F32),
        in_specs=[VMEM_SPEC],
        out_specs=VMEM_SPEC,
    )(jnp.pad(time_bias, ((0, 0), (0, 1))))
    depth = width // blocks
    wides = [count * TILE for _, count, _ in plan]
    wides[0] += LANES
    step = min(CHUNK, held)
    compute = pl.pallas_call(
        functools.partial(compute_kernel, frames, heads),
        out_shape=[
            jax.ShapeDtypeStruct((held, width), BF16),
            jax.ShapeDtypeStruct((width, held), BF16),
            jax.ShapeDtypeStruct((width, held), BF16),
            jax.ShapeDtypeStruct((held, 4 * width), BF16),
            jax.ShapeDtypeStruct((LANES, width), F32),
        ],
        in_specs=[VMEM_SPEC] * 8,
        out_specs=[VMEM_SPEC] * 5,
        scratch_shapes=[
            pltpu.VMEM((held, held), BF16),
            pltpu.VMEM((step, 3 * width), BF16),
            pltpu.VMEM((step, width), BF16),
            pltpu.VMEM((step, width), F32),
            pltpu.VMEM((step, width), F32),
            pltpu.VMEM((held, width), BF16),
        ],
        compiler_params=pltpu.CompilerParams(vmem_limit_bytes=52 * 2**20),
        cost_estimate=pl.CostEstimate(
            flops=30 * held * width * width, bytes_accessed=24 * 2**20, transcendentals=0
        ),
    )
    results, saved = [], []
    for half in range(2):
        got = lax.all_to_all(
            joint[half].reshape(seq, 2 * local_frames * part, width),
            "seq", split_axis=0, concat_axis=0, tiled=True,
        )
        result, *kept = compute(
            got.reshape(2 * held, width),
            rows,
            here.reshape(1, held),
            ln_gain.reshape(1, width),
            ln_bias.reshape(1, width),
            w_qkv,
            w_out,
            table,
        )
        saved.append(kept)
        results.append(
            lax.all_to_all(
                result.reshape(seq, local_frames * part, width),
                "seq", split_axis=0, concat_axis=0, tiled=True,
            )
        )
    terms = pl.pallas_call(
        functools.partial(weight_kernel, blocks, plan, scale),
        out_shape=[jax.ShapeDtypeStruct((blocks, depth, wide), BF16) for wide in wides],
        in_specs=[VMEM_SPEC] * 8,
        out_specs=[VMEM_SPEC] * 3,
        compiler_params=pltpu.CompilerParams(vmem_limit_bytes=40 * 2**20),
    )(*[saved[half][i] for i in range(4) for half in range(2)])
    if kernel_sum:
        orders = [order for _, _, order in plan]
        stages = len(orders[0])
        sums = pl.pallas_call(
            functools.partial(reduce_kernel, rep, orders),
            out_shape=[jax.ShapeDtypeStruct((depth, wide), F32) for wide in wides],
            in_specs=[VMEM_SPEC] * 3,
            out_specs=[VMEM_SPEC] * 3,
            scratch_shapes=[pltpu.VMEM((blocks // 2, depth, wide), BF16) for wide in wides]
            + [pltpu.VMEM((blocks, depth, wide), BF16) for wide in wides]
            + [pltpu.SemaphoreType.DMA((3, stages)), pltpu.SemaphoreType.DMA((3, stages))],
            compiler_params=pltpu.CompilerParams(
                collective_id=0, has_side_effects=True, vmem_limit_bytes=48 * 2**20
            ),
        )(*terms)
    else:
        sums = [
            lax.psum_scatter(
                term.reshape(width, -1).astype(F32), ("seq", "rep"), scatter_dimension=0, tiled=True
            )
            for term in terms
        ]
    results[1], sums = lax.optimization_barrier((results[1], sums))
    in_grad = pl.pallas_call(
        functools.partial(restore_kernel, local_frames),
        out_shape=jax.ShapeDtypeStruct((local_frames, patches, width), BF16),
        in_specs=[VMEM_SPEC] * 3,
        out_specs=VMEM_SPEC,
        compiler_params=pltpu.CompilerParams(vmem_limit_bytes=32 * 2**20),
    )(
        results[0].reshape(held, width),
        results[1].reshape(held, width),
        jnp.asarray(row_places(1, local_frames, group, positions)),
    )[None]
    first = wides[0] - LANES
    joined = jnp.concatenate([sums[0][:, :first], sums[1], sums[2]], axis=1)
    return (
        in_grad,
        joined[:, : 3 * width],
        joined[:, 3 * width :],
        sums[0][:, first],
        sums[0][:, first + 1],
    )


def solution(mesh):
    return jax.shard_map(
        on_device,
        mesh=mesh,
        in_specs=(
            P("rep", "seq", None, None),
            P("rep", "seq", None, None),
            P("rep", None),
            P(),
            P(),
            P(),
            P(),
            P(),
        ),
        out_specs=(
            P("rep", "seq", None, None),
            P(("seq", "rep"), None),
            P(("seq", "rep"), None),
            P(("seq", "rep")),
            P(("seq", "rep")),
        ),
        check_vma=False,
    )
```

```python
import functools

import jax
import jax.numpy as jnp
import numpy as np
from jax import lax
from jax.experimental import pallas as pl
from jax.experimental.pallas import tpu as pltpu
from jax.sharding import PartitionSpec as P

MESH = pl.DeviceIdType.MESH
CHUNK = 512
TILE = 256
LANES = 128
F32 = jnp.float32
BF16 = jnp.bfloat16


def dot_nn(a, b):
    return jnp.dot(a, b, preferred_element_type=F32)


def dot_nt(a, b):
    return lax.dot_general(a, b, (((1,), (1,)), ((), ())), preferred_element_type=F32)


def dot_tn(a, b):
    return lax.dot_general(a, b, (((0,), (0,)), ((), ())), preferred_element_type=F32)


def block_place(block, order):
    place = 0
    for bit in order:
        place = place * 2 + ((block >> bit) & 1)
    return place


def part_plan(model_width, blocks):
    tiles = 4 * model_width // TILE
    bits = blocks.bit_length() - 1
    rest = list(range(1, bits))
    first = tiles * 3 // 8
    if bits == 5:
        turns = [[1, 2, 3, 4], [2, 3, 1, 4], [3, 1, 4, 2]]
    else:
        turns = [rest[start:] + rest[:start] for start in range(3)]
    orders = [([0] if bits else []) + turn for turn in turns]
    return [
        (0, first, orders[0]),
        (first, first, orders[1]),
        (2 * first, tiles - 2 * first, orders[2]),
    ]


def arrange_kernel(local_frames, x_ref, g_ref, place_ref, first_ref, second_ref):
    group = place_ref.shape[1] // (2 * local_frames)
    count = place_ref.shape[1]
    spot = lax.broadcasted_iota(jnp.int32, (count, count), 0)
    pick = jnp.where(place_ref[...] == spot, 1.0, 0.0).astype(BF16)
    for g in range(x_ref.shape[1] // group):
        rows = [ref[f, g * group : (g + 1) * group, :] for ref in (x_ref, g_ref) for f in range(local_frames)]
        value = dot_nn(pick, jnp.concatenate(rows, axis=0)).astype(BF16)
        half = count // 2
        first_ref[g * half : (g + 1) * half, :] = value[:half]
        second_ref[g * half : (g + 1) * half, :] = value[half:]


def restore_kernel(local_frames, first_ref, second_ref, place_ref, out_ref):
    count = place_ref.shape[1]
    group, half = count // local_frames, count // 2
    spot = lax.broadcasted_iota(jnp.int32, (count, count), 0)
    pick = jnp.where(place_ref[...] == spot, 1.0, 0.0).astype(BF16)
    for g in range(out_ref.shape[1] // group):
        rows = [ref[g * half : (g + 1) * half, :] for ref in (first_ref, second_ref)]
        value = dot_tn(pick, jnp.concatenate(rows, axis=0)).astype(BF16)
        for f in range(local_frames):
            out_ref[f, g * group : (g + 1) * group, :] = value[f * group : (f + 1) * group]


def row_places(sources, local_frames, group, positions):
    part = positions // 2
    owners = group // positions
    s, f, at = np.meshgrid(np.arange(sources), np.arange(local_frames), np.arange(group), indexing="ij")
    owner, half, p = at // positions, at % positions // part, at % part
    place = (((half * owners + owner) * sources + s) * local_frames + f) * part + p
    return place.reshape(1, -1).astype(np.int32)


def table_kernel(frames, tb_ref, table):
    heads = tb_ref.shape[0]
    span = 2 * frames
    for h in range(heads):
        row = jnp.broadcast_to(tb_ref[h : h + 1, :], (frames, span))
        rolled = pltpu.roll(row, frames + 1, 1, stride=1, stride_axis=0)
        side = (h % 2) * frames
        table[h // 2, :, side : side + frames] = rolled[:, :frames]


def compute_kernel(
    frames, heads,
    x_ref, rows_ref, back_ref, gain_ref, bias_ref, wqkv_ref, wout_ref, table,
    out_ref, hidden_t, grad_t, z, extra,
    xsel, proj, agrad, hg, normed, res, sums,
):
    arrived, width = x_ref.shape
    tokens = back_ref.shape[1]
    step = min(CHUNK, tokens)
    per = step // frames
    head_dim = width // heads
    factor = head_dim ** (-0.5)
    pairs = heads // 2

    sums[...] = jnp.zeros_like(sums)
    lane = lax.broadcasted_iota(jnp.int32, (1, LANES), 1)
    left = (lane < head_dim).astype(BF16)
    right = (lane >= head_dim).astype(BF16)
    is_left = lane < head_dim

    def chunk(c, carry):
        base = pl.multiple_of(c * step, step)
        here = pl.ds(base, step)
        spot = lax.broadcasted_iota(jnp.int32, (step, tokens), 0) + base
        xsel[here, :] = jnp.where(back_ref[...] == spot, 1.0, 0.0).astype(BF16)
        want = lax.broadcasted_iota(jnp.int32, (step, arrived), 0) + base
        pick = jnp.where(rows_ref[0:1, :] == want, 1.0, 0.0).astype(BF16)
        x = dot_nn(pick, x_ref[...])
        mean = jnp.mean(x, axis=-1, keepdims=True)
        centred = x - mean
        inv = lax.rsqrt(jnp.mean(centred * centred, axis=-1, keepdims=True) + 1e-05)
        norm = centred * inv
        normed[...] = norm
        hidden_f = norm * gain_ref[...] + bias_ref[...]
        hidden = hidden_f.astype(BF16)
        hidden_t[:, here] = jnp.transpose(hidden_f).astype(BF16)

        pick_g = jnp.where(rows_ref[1:2, :] == want, 1.0, 0.0).astype(BF16)
        grad_f = dot_nn(pick_g, x_ref[...])
        grad = grad_f.astype(BF16)
        grad_t[:, here] = jnp.transpose(grad_f).astype(BF16)

        def project(j, carry):
            cols = pl.ds(pl.multiple_of(j * TILE, TILE), TILE)
            proj[:, cols] = dot_nn(hidden, wqkv_ref[:, cols]).astype(BF16)
            return carry

        lax.fori_loop(0, 3 * width // TILE, project, 0)

        def back(j, carry):
            cols = pl.ds(pl.multiple_of(j * TILE, TILE), TILE)
            agrad[:, cols] = dot_nt(grad, wout_ref[cols, :]).astype(BF16)
            return carry

        lax.fori_loop(0, width // TILE, back, 0)

        def attend(j, carry):
            at = pl.multiple_of(j * LANES, LANES)
            loaded, scored, soft = [], [], []
            for p in range(per):
                rows = slice(p * frames, (p + 1) * frames)
                q = proj[rows, pl.ds(at, LANES)]
                k = proj[rows, pl.ds(width + at, LANES)]
                v = proj[rows, pl.ds(2 * width + at, LANES)]
                da = agrad[rows, pl.ds(at, LANES)]
                kk = jnp.concatenate([k * left, k * right], axis=0)
                vv = jnp.concatenate([v * left, v * right], axis=0)
                loaded.append((q, da, kk, vv))
                scored.append((dot_nt(q, kk), dot_nt(da, vv)))
            for scores, wgrad in scored:
                scores = scores * factor + table[j]
                weights, sgrads = [], []
                for side in range(2):
                    s = scores[:, side * frames : (side + 1) * frames]
                    e = jnp.exp(s - jnp.max(s, axis=-1, keepdims=True))
                    w = e * (1.0 / jnp.sum(e, axis=-1, keepdims=True))
                    d = wgrad[:, side * frames : (side + 1) * frames]
                    inner = jnp.sum(d * w, axis=-1, keepdims=True)
                    weights.append(w.astype(BF16))
                    sgrads.append((w * (d - inner) * factor).astype(BF16))
                soft.append((jnp.concatenate(weights, axis=1), jnp.concatenate(sgrads, axis=1)))
            for p in range(per):
                (q, da, kk, vv), (w2, s2) = loaded[p], soft[p]
                there = pl.ds(base + p * frames, frames)
                z[there, pl.ds(3 * width + at, LANES)] = dot_nn(w2, vv).astype(BF16)
                z[there, pl.ds(at, LANES)] = dot_nn(s2, kk).astype(BF16)
                dk = dot_tn(s2, q)
                dv = dot_tn(w2, da)
                z[there, pl.ds(width + at, LANES)] = jnp.where(
                    is_left, dk[:frames], dk[frames:]
                ).astype(BF16)
                z[there, pl.ds(2 * width + at, LANES)] = jnp.where(
                    is_left, dv[:frames], dv[frames:]
                ).astype(BF16)
            return carry

        lax.fori_loop(0, pairs, attend, 0)

        def widen(j, carry):
            cols = pl.ds(pl.multiple_of(j * TILE, TILE), TILE)
            hg[:, cols] = dot_nt(z[here, : 3 * width], wqkv_ref[cols, :])
            return carry

        lax.fori_loop(0, width // TILE, widen, 0)
        hgrad = hg[...]
        norm = normed[...]
        sums[0:1, :] += jnp.sum(hgrad * norm, axis=0, keepdims=True)
        sums[1:2, :] += jnp.sum(hgrad, axis=0, keepdims=True)
        sc = hgrad * gain_ref[...]
        ngrad = inv * (
            sc
            - jnp.mean(sc, axis=-1, keepdims=True)
            - norm * jnp.mean(sc * norm, axis=-1, keepdims=True)
        )
        res[here, :] = (grad_f + ngrad).astype(BF16)
        return carry

    lax.fori_loop(0, tokens // step, chunk, 0)
    extra[...] = jnp.transpose(sums[...])

    def give_back(j, carry):
        cols = pl.ds(pl.multiple_of(j * TILE, TILE), TILE)
        out_ref[:, cols] = dot_tn(xsel[...], res[:, cols]).astype(BF16)
        return carry

    lax.fori_loop(0, width // TILE, give_back, 0)


def weight_part(blocks, plan, scale, part, sources, ref):
    hidden, grads, zs, extras = (sources[i : i + 2] for i in range(0, 8, 2))
    width = hidden[0].shape[0]
    depth = width // blocks
    hidden_tiles = 3 * width // TILE
    first, count, order = plan[part]
    for lo, hi, lhs in (
        (first, min(first + count, hidden_tiles), hidden),
        (max(first, hidden_tiles), first + count, grads),
    ):
        if hi <= lo:
            continue

        def term(j, carry, lhs=lhs):
            cols = pl.ds(pl.multiple_of(j * TILE, TILE), TILE)
            both = [dot_nn(rows[...], z[:, cols]) for rows, z in zip(lhs, zs)]
            value = ((both[0] + both[1]) * scale).astype(BF16)
            to = pl.ds(pl.multiple_of((j - first) * TILE, TILE), TILE)
            for b in range(blocks):
                ref[block_place(b, order), :, to] = value[b * depth : (b + 1) * depth]
            return carry

        lax.fori_loop(lo, hi, term, 0)
    if part == 0:
        extra = ((extras[0][...] + extras[1][...]) * scale).astype(BF16)
        wide = count * TILE
        for b in range(blocks):
            ref[block_place(b, order), :, wide:] = extra[b * depth : (b + 1) * depth]


def weight_kernel(blocks, plan, scale, *refs):
    for part in range(3):
        weight_part(blocks, plan, scale, part, refs[:8], refs[8 + part])


def reduce_kernel(rep, blocks, plan, scale, *refs):
    orders = [order for _, _, order in plan]
    count = len(orders)
    sources, refs = refs[:8], refs[8:]
    outs, ins, work, land = (refs[i * count : (i + 1) * count] for i in range(4))
    send_sem, recv_sem = refs[4 * count :]
    seq_id, rep_id = lax.axis_index("seq"), lax.axis_index("rep")
    me = seq_id * rep + rep_id
    stages = len(orders[0])

    def partner(bit):
        other = me + (1 - 2 * (lax.div(me, 1 << bit) % 2)) * (1 << bit)
        return (lax.div(other, rep), lax.rem(other, rep))

    barrier = pltpu.get_barrier_semaphore()
    for bit in range(stages):
        pl.semaphore_signal(barrier, inc=1, device_id=partner(bit), device_id_type=MESH)
    pl.semaphore_wait(barrier, stages)

    copies = {}
    base = [0] * count
    keeps = {}

    def start(part, stage):
        bit = orders[part][stage]
        mine = lax.div(me, 1 << bit) % 2
        half = ins[part].shape[0] >> (stage + 1)
        source = ins[part] if stage == 0 else work[part]
        at = half * 2 - half
        keeps[part, stage] = base[part] + mine * half
        away = base[part] + (1 - mine) * half
        copy = pltpu.make_async_remote_copy(
            src_ref=source.at[pl.ds(away, half)],
            dst_ref=land[part].at[pl.ds(at, half)],
            send_sem=send_sem.at[part, stage],
            recv_sem=recv_sem.at[part, stage],
            device_id=partner(bit),
            device_id_type=MESH,
        )
        copy.start()
        copies[part, stage] = copy

    def finish(part, stage):
        half = ins[part].shape[0] >> (stage + 1)
        copies[part, stage].wait_recv()
        keep = keeps[part, stage]
        if half == 1:
            total = work[part][keep].astype(F32) + land[part][half].astype(F32)
            outs[part][...] = total
            return
        source = ins[part] if stage == 0 else work[part]
        to = 0 if stage == 0 else keep

        def add(i, carry):
            work[part][to + i] = source[keep + i] + land[part][half + i]
            return carry

        lax.fori_loop(0, half, add, 0)
        base[part] = to

    for part in range(count):
        weight_part(blocks, plan, scale, part, sources, ins[part])
        start(part, 0)
        if part:
            finish(part - 1, 0)
            start(part - 1, 1)
    finish(count - 1, 0)
    start(count - 1, 1)
    for stage in range(1, stages):
        for part in range(count):
            finish(part, stage)
            if stage + 1 < stages:
                start(part, stage + 1)
    for copy in copies.values():
        copy.wait_send()


VMEM_SPEC = pl.BlockSpec(memory_space=pltpu.VMEM)


def on_device(layer_input, out_grad, slot_frame, ln_gain, ln_bias, w_qkv, w_out, time_bias):
    seq, rep = lax.axis_size("seq"), lax.axis_size("rep")
    _, local_frames, patches, width = layer_input.shape
    frames, positions = local_frames * seq, patches // seq
    tokens = frames * positions
    heads = time_bias.shape[0]
    devices = seq * rep
    kernel_sum = width // devices >= 16
    blocks = devices if kernel_sum else 1
    plan = part_plan(width, blocks)
    scale = float(tokens * devices) ** (-0.5)
    part = positions // 2
    held = tokens // 2
    span = 2 * frames

    group = min(patches, 256 // local_frames)
    joint = pl.pallas_call(
        functools.partial(arrange_kernel, local_frames),
        out_shape=[jax.ShapeDtypeStruct((2 * held, width), BF16)] * 2,
        in_specs=[VMEM_SPEC] * 3,
        out_specs=[VMEM_SPEC] * 2,
        compiler_params=pltpu.CompilerParams(vmem_limit_bytes=32 * 2**20),
    )(
        layer_input[0],
        out_grad[0],
        jnp.asarray(row_places(2, local_frames, group, positions)),
    )
    slots = jnp.arange(frames, dtype=jnp.int32)
    shift = jnp.arange(part, dtype=jnp.int32) * frames

    def places(at):
        return (at[:, None] + shift[None]).reshape(seq, local_frames * part)

    here = places(slots)
    none = jnp.full_like(here, -1)
    rows = jnp.stack(
        [
            jnp.concatenate([here, none], axis=1).reshape(2 * held),
            jnp.concatenate([none, places(slot_frame[0])], axis=1).reshape(2 * held),
        ]
    )
    table = pl.pallas_call(
        functools.partial(table_kernel, frames),
        out_shape=jax.ShapeDtypeStruct((heads // 2, frames, span), F32),
        in_specs=[VMEM_SPEC],
        out_specs=VMEM_SPEC,
    )(jnp.pad(time_bias, ((0, 0), (0, 1))))
    depth = width // blocks
    wides = [count * TILE for _, count, _ in plan]
    wides[0] += LANES
    step = min(CHUNK, held)
    compute = pl.pallas_call(
        functools.partial(compute_kernel, frames, heads),
        out_shape=[
            jax.ShapeDtypeStruct((held, width), BF16),
            jax.ShapeDtypeStruct((width, held), BF16),
            jax.ShapeDtypeStruct((width, held), BF16),
            jax.ShapeDtypeStruct((held, 4 * width), BF16),
            jax.ShapeDtypeStruct((width, LANES), F32),
        ],
        in_specs=[VMEM_SPEC] * 8,
        out_specs=[VMEM_SPEC] * 5,
        scratch_shapes=[
            pltpu.VMEM((held, held), BF16),
            pltpu.VMEM((step, 3 * width), BF16),
            pltpu.VMEM((step, width), BF16),
            pltpu.VMEM((step, width), F32),
            pltpu.VMEM((step, width), F32),
            pltpu.VMEM((held, width), BF16),
            pltpu.VMEM((LANES, width), F32),
        ],
        compiler_params=pltpu.CompilerParams(vmem_limit_bytes=40 * 2**20),
        cost_estimate=pl.CostEstimate(
            flops=30 * held * width * width, bytes_accessed=24 * 2**20, transcendentals=0
        ),
    )
    results, saved = [], []
    for half in range(2):
        got = lax.all_to_all(
            joint[half].reshape(seq, 2 * local_frames * part, width),
            "seq", split_axis=0, concat_axis=0, tiled=True,
        )
        result, *kept = compute(
            got.reshape(2 * held, width),
            rows,
            here.reshape(1, held),
            ln_gain.reshape(1, width),
            ln_bias.reshape(1, width),
            w_qkv,
            w_out,
            table,
        )
        saved.append(kept)
        results.append(
            lax.all_to_all(
                result.reshape(seq, local_frames * part, width),
                "seq", split_axis=0, concat_axis=0, tiled=True,
            )
        )
    operands = [saved[half][i] for i in range(4) for half in range(2)]
    if kernel_sum:
        stages = len(plan[0][2])
        sums = pl.pallas_call(
            functools.partial(reduce_kernel, rep, blocks, plan, scale),
            out_shape=[jax.ShapeDtypeStruct((depth, wide), F32) for wide in wides],
            in_specs=[VMEM_SPEC] * 8,
            out_specs=[VMEM_SPEC] * 3,
            scratch_shapes=[pltpu.VMEM((blocks, depth, wide), BF16) for wide in wides]
            + [pltpu.VMEM((blocks // 2, depth, wide), BF16) for wide in wides]
            + [pltpu.VMEM((blocks, depth, wide), BF16) for wide in wides]
            + [pltpu.SemaphoreType.DMA((3, stages)), pltpu.SemaphoreType.DMA((3, stages))],
            compiler_params=pltpu.CompilerParams(
                collective_id=0, has_side_effects=True, vmem_limit_bytes=48 * 2**20
            ),
            cost_estimate=pl.CostEstimate(
                flops=8 * tokens * width * width, bytes_accessed=160 * 2**20, transcendentals=0
            ),
        )(*operands)
    else:
        terms = pl.pallas_call(
            functools.partial(weight_kernel, blocks, plan, scale),
            out_shape=[jax.ShapeDtypeStruct((blocks, depth, wide), BF16) for wide in wides],
            in_specs=[VMEM_SPEC] * 8,
            out_specs=[VMEM_SPEC] * 3,
            compiler_params=pltpu.CompilerParams(vmem_limit_bytes=40 * 2**20),
        )(*operands)
        sums = [
            lax.psum_scatter(
                term.reshape(width, -1).astype(F32), ("seq", "rep"), scatter_dimension=0, tiled=True
            )
            for term in terms
        ]
    results[1], sums = lax.optimization_barrier((results[1], sums))
    in_grad = pl.pallas_call(
        functools.partial(restore_kernel, local_frames),
        out_shape=jax.ShapeDtypeStruct((local_frames, patches, width), BF16),
        in_specs=[VMEM_SPEC] * 3,
        out_specs=VMEM_SPEC,
        compiler_params=pltpu.CompilerParams(vmem_limit_bytes=32 * 2**20),
    )(
        results[0].reshape(held, width),
        results[1].reshape(held, width),
        jnp.asarray(row_places(1, local_frames, group, positions)),
    )[None]
    first = wides[0] - LANES
    return (
        in_grad,
        jnp.concatenate([sums[0][:, :first], sums[1]], axis=1),
        sums[2],
        sums[0][:, first],
        sums[0][:, first + 1],
    )


def solution(mesh):
    return jax.shard_map(
        on_device,
        mesh=mesh,
        in_specs=(
            P("rep", "seq", None, None),
            P("rep", "seq", None, None),
            P("rep", None),
            P(),
            P(),
            P(),
            P(),
            P(),
        ),
        out_specs=(
            P("rep", "seq", None, None),
            P(("seq", "rep"), None),
            P(("seq", "rep"), None),
            P(("seq", "rep")),
            P(("seq", "rep")),
        ),
        check_vma=False,
    )
```

```python
import functools

import jax
import jax.numpy as jnp
import numpy as np
from jax import lax
from jax.experimental import pallas as pl
from jax.experimental.pallas import tpu as pltpu
from jax.sharding import PartitionSpec as P

MESH = pl.DeviceIdType.MESH
CHUNK = 512
TILE = 256
LANES = 128
F32 = jnp.float32
BF16 = jnp.bfloat16


def dot_nn(a, b):
    return jnp.dot(a, b, preferred_element_type=F32)


def dot_nt(a, b):
    return lax.dot_general(a, b, (((1,), (1,)), ((), ())), preferred_element_type=F32)


def dot_tn(a, b):
    return lax.dot_general(a, b, (((0,), (0,)), ((), ())), preferred_element_type=F32)


def block_place(block, order):
    place = 0
    for bit in order:
        place = place * 2 + ((block >> bit) & 1)
    return place


def part_plan(model_width, blocks):
    tiles = 4 * model_width // TILE
    bits = blocks.bit_length() - 1
    rest = list(range(1, bits))
    wide, narrow = tiles * 3 // 16, tiles // 8
    if bits == 5:
        turns = [[1, 2, 3, 4], [2, 3, 1, 4], [3, 1, 4, 2]]
    else:
        turns = [rest[start:] + rest[:start] for start in range(3)]
    orders = [([0] if bits else []) + turn for turn in turns]
    plan = []
    for group in range(2):
        plan.append((group * wide, wide, orders[0]))
        plan.append((2 * wide + group * wide, wide, orders[1]))
        plan.append((4 * wide + group * narrow, narrow, orders[2]))
    return plan


def arrange_kernel(local_frames, x_ref, g_ref, place_ref, first_ref, second_ref):
    group = place_ref.shape[1] // (2 * local_frames)
    count = place_ref.shape[1]
    spot = lax.broadcasted_iota(jnp.int32, (count, count), 0)
    pick = jnp.where(place_ref[...] == spot, 1.0, 0.0).astype(BF16)
    for g in range(x_ref.shape[1] // group):
        rows = [ref[f, g * group : (g + 1) * group, :] for ref in (x_ref, g_ref) for f in range(local_frames)]
        value = dot_nn(pick, jnp.concatenate(rows, axis=0)).astype(BF16)
        half = count // 2
        first_ref[g * half : (g + 1) * half, :] = value[:half]
        second_ref[g * half : (g + 1) * half, :] = value[half:]


def restore_kernel(local_frames, first_ref, second_ref, place_ref, out_ref):
    count = place_ref.shape[1]
    group, half = count // local_frames, count // 2
    spot = lax.broadcasted_iota(jnp.int32, (count, count), 0)
    pick = jnp.where(place_ref[...] == spot, 1.0, 0.0).astype(BF16)
    for g in range(out_ref.shape[1] // group):
        rows = [ref[g * half : (g + 1) * half, :] for ref in (first_ref, second_ref)]
        value = dot_tn(pick, jnp.concatenate(rows, axis=0)).astype(BF16)
        for f in range(local_frames):
            out_ref[f, g * group : (g + 1) * group, :] = value[f * group : (f + 1) * group]


def row_places(sources, local_frames, group, positions):
    part = positions // 2
    owners = group // positions
    s, f, at = np.meshgrid(np.arange(sources), np.arange(local_frames), np.arange(group), indexing="ij")
    owner, half, p = at // positions, at % positions // part, at % part
    place = (((half * owners + owner) * sources + s) * local_frames + f) * part + p
    return place.reshape(1, -1).astype(np.int32)


def table_kernel(frames, tb_ref, table):
    heads = tb_ref.shape[0]
    span = 2 * frames
    for h in range(heads):
        row = jnp.broadcast_to(tb_ref[h : h + 1, :], (frames, span))
        rolled = pltpu.roll(row, frames + 1, 1, stride=1, stride_axis=0)
        side = (h % 2) * frames
        table[h // 2, :, side : side + frames] = rolled[:, :frames]


def compute_kernel(
    frames, heads,
    x_ref, rows_ref, back_ref, gain_ref, bias_ref, wqkv_ref, wout_ref, table,
    out_ref, hidden_t, grad_t, z, extra,
    xsel, proj, agrad, hg, normed, res, sums,
):
    arrived, width = x_ref.shape
    tokens = back_ref.shape[1]
    step = min(CHUNK, tokens)
    per = step // frames
    head_dim = width // heads
    factor = head_dim ** (-0.5)
    pairs = heads // 2

    sums[...] = jnp.zeros_like(sums)
    lane = lax.broadcasted_iota(jnp.int32, (1, LANES), 1)
    left = (lane < head_dim).astype(BF16)
    right = (lane >= head_dim).astype(BF16)
    is_left = lane < head_dim

    def chunk(c, carry):
        base = pl.multiple_of(c * step, step)
        here = pl.ds(base, step)
        spot = lax.broadcasted_iota(jnp.int32, (step, tokens), 0) + base
        xsel[here, :] = jnp.where(back_ref[...] == spot, 1.0, 0.0).astype(BF16)
        want = lax.broadcasted_iota(jnp.int32, (step, arrived), 0) + base
        pick = jnp.where(rows_ref[0:1, :] == want, 1.0, 0.0).astype(BF16)
        x = dot_nn(pick, x_ref[...])
        mean = jnp.mean(x, axis=-1, keepdims=True)
        centred = x - mean
        inv = lax.rsqrt(jnp.mean(centred * centred, axis=-1, keepdims=True) + 1e-05)
        norm = centred * inv
        normed[...] = norm
        hidden_f = norm * gain_ref[...] + bias_ref[...]
        hidden = hidden_f.astype(BF16)
        hidden_t[:, here] = jnp.transpose(hidden_f).astype(BF16)

        pick_g = jnp.where(rows_ref[1:2, :] == want, 1.0, 0.0).astype(BF16)
        grad_f = dot_nn(pick_g, x_ref[...])
        grad = grad_f.astype(BF16)
        grad_t[:, here] = jnp.transpose(grad_f).astype(BF16)

        def project(j, carry):
            cols = pl.ds(pl.multiple_of(j * TILE, TILE), TILE)
            proj[:, cols] = dot_nn(hidden, wqkv_ref[:, cols]).astype(BF16)
            return carry

        lax.fori_loop(0, 3 * width // TILE, project, 0)

        def back(j, carry):
            cols = pl.ds(pl.multiple_of(j * TILE, TILE), TILE)
            agrad[:, cols] = dot_nt(grad, wout_ref[cols, :]).astype(BF16)
            return carry

        lax.fori_loop(0, width // TILE, back, 0)

        def attend(j, carry):
            at = pl.multiple_of(j * LANES, LANES)
            loaded, scored, soft = [], [], []
            for p in range(per):
                rows = slice(p * frames, (p + 1) * frames)
                q = proj[rows, pl.ds(at, LANES)]
                k = proj[rows, pl.ds(width + at, LANES)]
                v = proj[rows, pl.ds(2 * width + at, LANES)]
                da = agrad[rows, pl.ds(at, LANES)]
                kk = jnp.concatenate([k * left, k * right], axis=0)
                vv = jnp.concatenate([v * left, v * right], axis=0)
                loaded.append((q, da, kk, vv))
                scored.append((dot_nt(q, kk), dot_nt(da, vv)))
            for scores, wgrad in scored:
                scores = scores * factor + table[j]
                weights, sgrads = [], []
                for side in range(2):
                    s = scores[:, side * frames : (side + 1) * frames]
                    e = jnp.exp(s - jnp.max(s, axis=-1, keepdims=True))
                    w = e * (1.0 / jnp.sum(e, axis=-1, keepdims=True))
                    d = wgrad[:, side * frames : (side + 1) * frames]
                    inner = jnp.sum(d * w, axis=-1, keepdims=True)
                    weights.append(w.astype(BF16))
                    sgrads.append((w * (d - inner) * factor).astype(BF16))
                soft.append((jnp.concatenate(weights, axis=1), jnp.concatenate(sgrads, axis=1)))
            for p in range(per):
                (q, da, kk, vv), (w2, s2) = loaded[p], soft[p]
                there = pl.ds(base + p * frames, frames)
                z[there, pl.ds(3 * width + at, LANES)] = dot_nn(w2, vv).astype(BF16)
                z[there, pl.ds(at, LANES)] = dot_nn(s2, kk).astype(BF16)
                dk = dot_tn(s2, q)
                dv = dot_tn(w2, da)
                z[there, pl.ds(width + at, LANES)] = jnp.where(
                    is_left, dk[:frames], dk[frames:]
                ).astype(BF16)
                z[there, pl.ds(2 * width + at, LANES)] = jnp.where(
                    is_left, dv[:frames], dv[frames:]
                ).astype(BF16)
            return carry

        lax.fori_loop(0, pairs, attend, 0)

        def widen(j, carry):
            cols = pl.ds(pl.multiple_of(j * TILE, TILE), TILE)
            hg[:, cols] = dot_nt(z[here, : 3 * width], wqkv_ref[cols, :])
            return carry

        lax.fori_loop(0, width // TILE, widen, 0)
        hgrad = hg[...]
        norm = normed[...]
        sums[0:1, :] += jnp.sum(hgrad * norm, axis=0, keepdims=True)
        sums[1:2, :] += jnp.sum(hgrad, axis=0, keepdims=True)
        sc = hgrad * gain_ref[...]
        ngrad = inv * (
            sc
            - jnp.mean(sc, axis=-1, keepdims=True)
            - norm * jnp.mean(sc * norm, axis=-1, keepdims=True)
        )
        res[here, :] = (grad_f + ngrad).astype(BF16)
        return carry

    lax.fori_loop(0, tokens // step, chunk, 0)
    extra[...] = jnp.transpose(sums[...])

    def give_back(j, carry):
        cols = pl.ds(pl.multiple_of(j * TILE, TILE), TILE)
        out_ref[:, cols] = dot_tn(xsel[...], res[:, cols]).astype(BF16)
        return carry

    lax.fori_loop(0, width // TILE, give_back, 0)


def weight_part(blocks, plan, scale, part, sources, ref):
    hidden, grads, zs, extras = (sources[i : i + 2] for i in range(0, 8, 2))
    width = hidden[0].shape[0]
    depth = width // blocks
    hidden_tiles = 3 * width // TILE
    first, count, order = plan[part]
    for lo, hi, lhs in (
        (first, min(first + count, hidden_tiles), hidden),
        (max(first, hidden_tiles), first + count, grads),
    ):
        if hi <= lo:
            continue

        def term(j, carry, lhs=lhs):
            cols = pl.ds(pl.multiple_of(j * TILE, TILE), TILE)
            both = [dot_nn(rows[...], z[:, cols]) for rows, z in zip(lhs, zs)]
            value = ((both[0] + both[1]) * scale).astype(BF16)
            to = pl.ds(pl.multiple_of((j - first) * TILE, TILE), TILE)
            for b in range(blocks):
                ref[block_place(b, order), :, to] = value[b * depth : (b + 1) * depth]
            return carry

        lax.fori_loop(lo, hi, term, 0)
    if part == 0:
        extra = ((extras[0][...] + extras[1][...]) * scale).astype(BF16)
        wide = count * TILE
        for b in range(blocks):
            ref[block_place(b, order), :, wide:] = extra[b * depth : (b + 1) * depth]


def weight_kernel(blocks, plan, scale, *refs):
    for part in range(len(plan)):
        weight_part(blocks, plan, scale, part, refs[:8], refs[8 + part])


def reduce_kernel(rep, blocks, plan, scale, *refs):
    orders = [order for _, _, order in plan]
    count = len(orders)
    sources, refs = refs[:8], refs[8:]
    outs, ins, work, land = (refs[i * count : (i + 1) * count] for i in range(4))
    send_sem, recv_sem = refs[4 * count :]
    seq_id, rep_id = lax.axis_index("seq"), lax.axis_index("rep")
    me = seq_id * rep + rep_id
    stages = len(orders[0])

    def partner(bit):
        other = me + (1 - 2 * (lax.div(me, 1 << bit) % 2)) * (1 << bit)
        return (lax.div(other, rep), lax.rem(other, rep))

    barrier = pltpu.get_barrier_semaphore()
    for bit in range(stages):
        pl.semaphore_signal(barrier, inc=1, device_id=partner(bit), device_id_type=MESH)
    pl.semaphore_wait(barrier, stages)

    copies = {}
    base = [0] * count
    keeps = {}

    def start(part, stage):
        bit = orders[part][stage]
        mine = lax.div(me, 1 << bit) % 2
        half = ins[part].shape[0] >> (stage + 1)
        source = ins[part] if stage == 0 else work[part]
        at = half * 2 - half
        keeps[part, stage] = base[part] + mine * half
        away = base[part] + (1 - mine) * half
        copy = pltpu.make_async_remote_copy(
            src_ref=source.at[pl.ds(away, half)],
            dst_ref=land[part].at[pl.ds(at, half)],
            send_sem=send_sem.at[part, stage],
            recv_sem=recv_sem.at[part, stage],
            device_id=partner(bit),
            device_id_type=MESH,
        )
        copy.start()
        copies[part, stage] = copy

    def finish(part, stage):
        half = ins[part].shape[0] >> (stage + 1)
        copies[part, stage].wait_recv()
        keep = keeps[part, stage]
        if half == 1:
            total = work[part][keep].astype(F32) + land[part][half].astype(F32)
            outs[part][...] = total
            return
        source = ins[part] if stage == 0 else work[part]
        to = 0 if stage == 0 else keep

        def add(i, carry):
            work[part][to + i] = source[keep + i] + land[part][half + i]
            return carry

        lax.fori_loop(0, half, add, 0)
        base[part] = to

    for part in range(count):
        weight_part(blocks, plan, scale, part, sources, ins[part])
        start(part, 0)
        if part:
            finish(part - 1, 0)
            start(part - 1, 1)
    finish(count - 1, 0)
    start(count - 1, 1)
    for stage in range(1, stages):
        for part in range(count):
            finish(part, stage)
            if stage + 1 < stages:
                start(part, stage + 1)
    for copy in copies.values():
        copy.wait_send()


VMEM_SPEC = pl.BlockSpec(memory_space=pltpu.VMEM)


def on_device(layer_input, out_grad, slot_frame, ln_gain, ln_bias, w_qkv, w_out, time_bias):
    seq, rep = lax.axis_size("seq"), lax.axis_size("rep")
    _, local_frames, patches, width = layer_input.shape
    frames, positions = local_frames * seq, patches // seq
    tokens = frames * positions
    heads = time_bias.shape[0]
    devices = seq * rep
    kernel_sum = width // devices >= 16
    blocks = devices if kernel_sum else 1
    plan = part_plan(width, blocks)
    scale = float(tokens * devices) ** (-0.5)
    part = positions // 2
    held = tokens // 2
    span = 2 * frames

    group = min(patches, 256 // local_frames)
    joint = pl.pallas_call(
        functools.partial(arrange_kernel, local_frames),
        out_shape=[jax.ShapeDtypeStruct((2 * held, width), BF16)] * 2,
        in_specs=[VMEM_SPEC] * 3,
        out_specs=[VMEM_SPEC] * 2,
        compiler_params=pltpu.CompilerParams(vmem_limit_bytes=32 * 2**20),
    )(
        layer_input[0],
        out_grad[0],
        jnp.asarray(row_places(2, local_frames, group, positions)),
    )
    slots = jnp.arange(frames, dtype=jnp.int32)
    shift = jnp.arange(part, dtype=jnp.int32) * frames

    def places(at):
        return (at[:, None] + shift[None]).reshape(seq, local_frames * part)

    here = places(slots)
    none = jnp.full_like(here, -1)
    rows = jnp.stack(
        [
            jnp.concatenate([here, none], axis=1).reshape(2 * held),
            jnp.concatenate([none, places(slot_frame[0])], axis=1).reshape(2 * held),
        ]
    )
    table = pl.pallas_call(
        functools.partial(table_kernel, frames),
        out_shape=jax.ShapeDtypeStruct((heads // 2, frames, span), F32),
        in_specs=[VMEM_SPEC],
        out_specs=VMEM_SPEC,
    )(jnp.pad(time_bias, ((0, 0), (0, 1))))
    depth = width // blocks
    wides = [count * TILE for _, count, _ in plan]
    wides[0] += LANES
    step = min(CHUNK, held)
    compute = pl.pallas_call(
        functools.partial(compute_kernel, frames, heads),
        out_shape=[
            jax.ShapeDtypeStruct((held, width), BF16),
            jax.ShapeDtypeStruct((width, held), BF16),
            jax.ShapeDtypeStruct((width, held), BF16),
            jax.ShapeDtypeStruct((held, 4 * width), BF16),
            jax.ShapeDtypeStruct((width, LANES), F32),
        ],
        in_specs=[VMEM_SPEC] * 8,
        out_specs=[VMEM_SPEC] * 5,
        scratch_shapes=[
            pltpu.VMEM((held, held), BF16),
            pltpu.VMEM((step, 3 * width), BF16),
            pltpu.VMEM((step, width), BF16),
            pltpu.VMEM((step, width), F32),
            pltpu.VMEM((step, width), F32),
            pltpu.VMEM((held, width), BF16),
            pltpu.VMEM((LANES, width), F32),
        ],
        compiler_params=pltpu.CompilerParams(vmem_limit_bytes=56 * 2**20),
        cost_estimate=pl.CostEstimate(
            flops=30 * held * width * width, bytes_accessed=24 * 2**20, transcendentals=0
        ),
    )
    results, saved = [], []
    for half in range(2):
        got = lax.all_to_all(
            joint[half].reshape(seq, 2 * local_frames * part, width),
            "seq", split_axis=0, concat_axis=0, tiled=True,
        )
        result, *kept = compute(
            got.reshape(2 * held, width),
            rows,
            here.reshape(1, held),
            ln_gain.reshape(1, width),
            ln_bias.reshape(1, width),
            w_qkv,
            w_out,
            table,
        )
        saved.append(kept)
        results.append(
            lax.all_to_all(
                result.reshape(seq, local_frames * part, width),
                "seq", split_axis=0, concat_axis=0, tiled=True,
            )
        )
    operands = [saved[half][i] for i in range(4) for half in range(2)]
    if kernel_sum:
        stages = len(plan[0][2])
        sums = pl.pallas_call(
            functools.partial(reduce_kernel, rep, blocks, plan, scale),
            out_shape=[jax.ShapeDtypeStruct((depth, wide), F32) for wide in wides],
            in_specs=[VMEM_SPEC] * 8,
            out_specs=[VMEM_SPEC] * len(plan),
            scratch_shapes=[pltpu.VMEM((blocks, depth, wide), BF16) for wide in wides]
            + [pltpu.VMEM((blocks // 2, depth, wide), BF16) for wide in wides]
            + [pltpu.VMEM((blocks, depth, wide), BF16) for wide in wides]
            + [pltpu.SemaphoreType.DMA((len(plan), stages))] * 2,
            compiler_params=pltpu.CompilerParams(
                collective_id=0, has_side_effects=True, vmem_limit_bytes=58 * 2**20
            ),
            cost_estimate=pl.CostEstimate(
                flops=8 * tokens * width * width, bytes_accessed=160 * 2**20, transcendentals=0
            ),
        )(*operands)
    else:
        terms = pl.pallas_call(
            functools.partial(weight_kernel, blocks, plan, scale),
            out_shape=[jax.ShapeDtypeStruct((blocks, depth, wide), BF16) for wide in wides],
            in_specs=[VMEM_SPEC] * 8,
            out_specs=[VMEM_SPEC] * len(plan),
            compiler_params=pltpu.CompilerParams(vmem_limit_bytes=40 * 2**20),
        )(*operands)
        sums = [
            lax.psum_scatter(
                term.reshape(width, -1).astype(F32), ("seq", "rep"), scatter_dimension=0, tiled=True
            )
            for term in terms
        ]
    results[1], sums = lax.optimization_barrier((results[1], sums))
    in_grad = pl.pallas_call(
        functools.partial(restore_kernel, local_frames),
        out_shape=jax.ShapeDtypeStruct((local_frames, patches, width), BF16),
        in_specs=[VMEM_SPEC] * 3,
        out_specs=VMEM_SPEC,
        compiler_params=pltpu.CompilerParams(vmem_limit_bytes=32 * 2**20),
    )(
        results[0].reshape(held, width),
        results[1].reshape(held, width),
        jnp.asarray(row_places(1, local_frames, group, positions)),
    )[None]
    first = wides[0] - LANES
    return (
        in_grad,
        jnp.concatenate([sums[0][:, :first], sums[3], sums[1], sums[4]], axis=1),
        jnp.concatenate([sums[2], sums[5]], axis=1),
        sums[0][:, first],
        sums[0][:, first + 1],
    )


def solution(mesh):
    return jax.shard_map(
        on_device,
        mesh=mesh,
        in_specs=(
            P("rep", "seq", None, None),
            P("rep", "seq", None, None),
            P("rep", None),
            P(),
            P(),
            P(),
            P(),
            P(),
        ),
        out_specs=(
            P("rep", "seq", None, None),
            P(("seq", "rep"), None),
            P(("seq", "rep"), None),
            P(("seq", "rep")),
            P(("seq", "rep")),
        ),
        check_vma=False,
    )
```
